256 devices in a mesh: spatial: 64 (over y, z, core), dp: 4 (over x).
Axes of the slice: x: 4, y: 4, z: 8, core: 2. Of those that a mesh axis runs over, the one named last changes fastest.
Arguments:
- features: bfloat16 [4, 384, 8, 8, 512], P('dp', 'spatial'), may hold values from -6 to 6
- masks: int32 [4, 384, 512], P('dp', 'spatial'), may hold values 0 or 1
- rulebook: int32 [4, 384, 27], P('dp', 'spatial'), may hold values from 0 to 134, as said below
- send_lists: int32 [4, 64, 64, 2], P('dp', 'spatial'), may hold values from 0 to 6, as said below
- conv_weight: bfloat16 [27, 64, 64], replicated, may hold values from -0.15625 to 0.15625
- down_weight: bfloat16 [8, 64, 128], replicated, may hold values from -0.25 to 0.25
- cotangent: bfloat16 [4, 384, 4, 4, 512], P('dp', 'spatial'), may hold values from -6 to 6
Outputs:
- coarse_out: bfloat16 [4, 384, 4, 4, 512], P('dp', 'spatial')
- grad_features: bfloat16 [4, 384, 8, 8, 512], P('dp', 'spatial')
- grad_conv: float32 [27, 64, 64], replicated
- grad_down: float32 [8, 64, 128], replicated
The draws below stay inside these ranges and needn't reach their ends.
Inputs may be any that keep to these rules, and one draw needn't show every extreme that they name: `send_lists`: with q = d // 16, device d of spatial is region ((q % 2) (2) + q // 2, (d // 4) % 4, d % 4) of a 4^3 grid without wrap. A device sends 2 distinct bricks to each region sharing a face with it, one brick (slot 0) to each sharing only an edge or a corner, and nothing to itself or to other regions; empty slots hold 6. Entries index the owning device's extended list; entry 13 of a brick is the brick's own local index; entries name only own bricks, filled received slots and 134, and each of these appears in the device's rulebook.
All inputs are finite; a program needn't handle non-finite values. No bound on the sum of `masks` on one device may be relied on, other than what follows from the above.
Results may differ from the reference program's by a relative error of at most 0.0095.
Values may be sent and summed in bfloat16 or wider, within the bound.
No kernel may reach another device: no remote copies, remote signals or barrier semaphores. Data moves between devices by JAX's collectives and lax.ppermute only.
A program may use at most 192 MiB of HBM per device.

```python
import jax
import jax.numpy as jnp
from jax import lax

C = 64
CO = 128
BR = 8
CAP = 2
BD = 6
SCENES = 4
NB = 384
HB = 4
SLOTS = 134
GRID = 4
N_SPATIAL = 64


def slot_counts():
    index = jnp.arange(N_SPATIAL, dtype=jnp.int32)
    slow = index // (GRID * GRID)
    first = slow % 2 * (GRID // 2) + slow // 2
    coords = jnp.stack([first, index // GRID % GRID, index % GRID], axis=1)
    apart = jnp.abs(coords[:, None, :] - coords[None, :, :])
    near = jnp.all(apart <= 1, axis=2)
    moved = jnp.sum((apart > 0).astype(jnp.int32), axis=2)
    counts = jnp.where(moved == 1, CAP, 1)
    return jnp.where(near & (moved > 0), counts, 0).astype(jnp.int32)


def draw_send_lists(key, part):
    scores = jax.random.randint(key, (SCENES, N_SPATIAL, N_SPATIAL, BD), 0, 2 ** 16) * BD + jnp.arange(BD, dtype=jnp.int32)
    order = jnp.argsort(scores, axis=-1, stable=True)[..., :CAP].astype(jnp.int32)
    counts = slot_counts()
    used = jnp.arange(CAP, dtype=jnp.int32)[None, None, None, :] < counts[None, :, :, None]
    return jnp.where(used, order, BD).astype(jnp.int32)


def draw_rulebook(key, part):
    span = SLOTS + 1
    total = 26 * BD
    extra = total - span
    groups = SCENES * N_SPATIAL
    key_pick, key_fill, key_empty, key_order = jax.random.split(jax.random.fold_in(key, 7), 4)
    counts = slot_counts()
    slot_used = jnp.arange(CAP, dtype=jnp.int32)[None, None, :] < counts[:, :, None]
    received = jnp.transpose(slot_used, (1, 0, 2)).reshape(N_SPATIAL, N_SPATIAL * CAP)
    valid = jnp.concatenate([jnp.ones((N_SPATIAL, BD), bool), received, jnp.ones((N_SPATIAL, 1), bool)], axis=1)
    sort_key = jnp.where(valid, 0, 1).astype(jnp.int32) * span + jnp.arange(span, dtype=jnp.int32)
    ordered = jnp.argsort(sort_key, axis=1, stable=True).astype(jnp.int32)
    number = jnp.sum(valid.astype(jnp.int32), axis=1)
    ordered = jnp.tile(ordered, (SCENES, 1))
    number = jnp.tile(number, (SCENES,))[:, None]
    fill_pick = jax.random.randint(key_fill, (groups, span), 0, 2 ** 16) % number
    position = jnp.arange(span, dtype=jnp.int32)[None, :]
    base_pos = jnp.where(position < number, position, fill_pick).astype(jnp.int32)
    base = jnp.take_along_axis(ordered, base_pos, axis=1)
    pick_pos = (jax.random.randint(key_pick, (groups, extra), 0, 2 ** 16) % number).astype(jnp.int32)
    picked = jnp.take_along_axis(ordered, pick_pos, axis=1)
    empty = jax.random.randint(key_empty, (groups, extra), 0, 3) == 0
    tail = jnp.where(empty, SLOTS, picked).astype(jnp.int32)
    entries = jnp.concatenate([base, tail], axis=1)
    scores = jax.random.randint(key_order, (groups, total), 0, 2 ** 16) * total + jnp.arange(total, dtype=jnp.int32)
    order = jnp.argsort(scores, axis=-1, stable=True)
    mixed = jnp.take_along_axis(entries, order, axis=1).reshape(groups, BD, 26)
    centre = jnp.broadcast_to(jnp.arange(BD, dtype=jnp.int32)[None, :, None], (groups, BD, 1))
    full = jnp.concatenate([mixed[:, :, :13], centre, mixed[:, :, 13:]], axis=2)
    return full.reshape(SCENES, NB, 27).astype(jnp.int32)


def touch_ends(array, rng, smallest, top_value):
    longest = array.shape.index(max(array.shape))
    spots = []
    for shift in (0, 1):
        where = [jax.random.randint(jax.random.fold_in(rng, axis), (), 0, length) for axis, length in enumerate(array.shape)]
        where[longest] = (where[longest] + shift) % array.shape[longest]
        spots.append(tuple(where))
    return array.at[spots[0]].set(smallest).at[spots[1]].set(top_value)


def levels(own_key, shape, cuts, low, top_value):
    gain, own = 1.0, jax.random.fold_in(own_key, 6)
    for dim, blocks in cuts:
        steps = jnp.exp(jax.random.uniform(jax.random.fold_in(own, dim), (blocks,), jnp.float32, low / len(cuts), top_value / len(cuts)))
        gain = gain * jnp.repeat(steps, shape[dim] // blocks).reshape([-1 if axis == dim else 1 for axis in range(len(shape))])
    return gain


def normal_values(rng, shape, deviation, most, cuts=(), kind=jnp.bfloat16):
    values = jax.random.normal(rng, shape, jnp.float32) * deviation
    if len(cuts) > 0:
        values = levels(rng, shape, cuts, -0.22, 0.18) * values
    return jnp.clip(values, min=-most, max=most).astype(kind)


def setup_inputs(seed: int = 0) -> dict:
    seeds = jax.random.split(jax.random.key(seed), 8)
    features = normal_values(seeds[0], (SCENES, NB, BR, BR, BR * C), 1.0, 6.0, ((0, 4), (1, 64)))
    masks = touch_ends((jax.random.randint(seeds[1], (SCENES, NB, BR**3), 0, 5) < 2).astype(jnp.int32), jax.random.fold_in(seeds[1], 1), 0, 1)
    rulebook = draw_rulebook(jax.random.fold_in(seeds[7], 71), 0)
    send_lists = draw_send_lists(jax.random.fold_in(seeds[7], 71), 0)
    conv_weight = normal_values(seeds[4], (27, C, C), (27 * C) ** -0.5, 0.15625)
    down_weight = normal_values(seeds[5], (8, C, CO), (8 * C) ** -0.5, 0.25)
    cotangent = normal_values(seeds[6], (SCENES, NB, HB, HB, HB * CO), 1.0, 6.0, ((0, 4), (1, 64)))
    return dict(features=features, masks=masks, rulebook=rulebook, send_lists=send_lists, conv_weight=conv_weight, down_weight=down_weight, cotangent=cotangent)


def rim_range(pos, edge):
    if pos == 0:
        return (edge - 1, edge)
    if pos == 1:
        return (0, edge)
    return (0, 1)

def assemble(extended, table, edge, width):
    planes = []
    for x_pos in range(3):
        rows = []
        for y_pos in range(3):
            cols = []
            for z_pos in range(3):
                x_lo, x_hi = rim_range(x_pos, edge)
                y_lo, y_hi = rim_range(y_pos, edge)
                z_lo, z_hi = rim_range(z_pos, edge)
                part = extended[:, x_lo:x_hi, y_lo:y_hi, z_lo * width:z_hi * width]
                cols.append(jnp.take(part, table[:, x_pos * 9 + y_pos * 3 + z_pos], axis=0))
            rows.append(jnp.concatenate(cols, axis=3))
        planes.append(jnp.concatenate(rows, axis=2))
    return jnp.concatenate(planes, axis=1)

def conv_split(padded, weights, edge, width):
    count = padded.shape[0]
    blocks = padded.reshape(count, edge + 2, edge + 2, edge + 2, width)
    total = jnp.zeros((count, edge, edge, edge, width), jnp.float32)
    for x_pos in range(3):
        for y_pos in range(3):
            for z_pos in range(3):
                piece = blocks[:, x_pos:x_pos + edge, y_pos:y_pos + edge, z_pos:z_pos + edge]
                total = total + jnp.einsum('nxyzi,io->nxyzo', piece, weights[x_pos * 9 + y_pos * 3 + z_pos])
    return total.reshape(count, edge, edge, edge * width)

def silu_grad(value):
    sig = jax.nn.sigmoid(value)
    return sig * (1.0 + value * (1.0 - sig))

def to_children(hidden, count, half, width):
    split = hidden.reshape(count, half, 2, half, 2, half, 2 * width)
    return split.transpose(0, 1, 3, 5, 2, 4, 6).reshape(count * half ** 3, 8 * width)

def from_children(grads, count, half, width):
    split = grads.reshape(count, half, half, half, 2, 2, 2 * width)
    return split.transpose(0, 1, 4, 2, 5, 3, 6).reshape(count, 2 * half, 2 * half, 2 * half * width)

def reference(features, masks, rulebook, send_lists, conv_weight, down_weight, cotangent):
    edge, width, half, peers, count, slots = (BR, C, HB, N_SPATIAL, BD, CAP)
    conv32 = conv_weight.astype(jnp.float32)
    flat_down = down_weight.reshape(8 * width, CO)
    scale = float(SCENES * NB * BR ** 3) ** (-0.5)
    conv_total = jnp.zeros((27, width, width), jnp.float32)
    down_total = jnp.zeros((8 * width, CO), jnp.float32)
    outputs = []
    grad_list = []
    for scene in range(SCENES):
        voxels = masks[scene].reshape(peers, count, edge, edge, edge)
        keep = jnp.repeat(voxels, width, axis=4).astype(jnp.bfloat16)
        masked = features[scene].reshape(peers, count, edge, edge, edge * width) * keep
        masked_ext = jnp.concatenate([masked, jnp.zeros((peers, 1, edge, edge, edge * width), jnp.bfloat16)], axis=1)
        tables = rulebook[scene].reshape(peers, count, 27)
        coarse_all = voxels.reshape(peers, count, half, 2, half, 2, half, 2).max(axis=(3, 5, 7))
        cot_all = cotangent[scene].reshape(peers, count * half ** 3, CO)
        sends = send_lists[scene]
        owners = jnp.arange(peers).astype(jnp.int32)[:, None]

        def device_step(carry, device):
            grads, conv_acc, down_acc = carry
            chosen = sends[:, device, :]
            arrived = masked_ext[owners, chosen].reshape(peers * slots, edge, edge, edge * width)
            extended = jnp.concatenate([masked[device], arrived, jnp.zeros((1, edge, edge, edge * width), jnp.bfloat16)], axis=0)
            table = tables[device]
            keep32 = keep[device].astype(jnp.float32)

            def hidden_map(ext32, weight32):
                return conv_split(assemble(ext32, table, edge, width), weight32, edge, width)
            raw, pullback = jax.vjp(hidden_map, extended.astype(jnp.float32), conv32)
            pre_hidden = raw * keep32
            hidden = jax.nn.silu(pre_hidden).astype(jnp.bfloat16)
            children = to_children(hidden, count, half, width)
            pre_out = jnp.dot(children, flat_down, preferred_element_type=jnp.float32)
            coarse = coarse_all[device].reshape(-1, 1).astype(jnp.float32)
            output = (jax.nn.silu(pre_out) * coarse).astype(jnp.bfloat16)
            grad_pre = (cot_all[device].astype(jnp.float32) * coarse * silu_grad(pre_out)).astype(jnp.bfloat16)
            down_part = jnp.dot(children.T, grad_pre, preferred_element_type=jnp.float32)
            grad_children = jnp.dot(grad_pre, flat_down.T, preferred_element_type=jnp.float32)
            grad_hidden = from_children(grad_children, count, half, width)
            grad_pre_hidden = (grad_hidden * silu_grad(pre_hidden) * keep32).astype(jnp.bfloat16)
            grad_ext, conv_part = pullback(grad_pre_hidden.astype(jnp.float32))
            returning = lax.optimization_barrier(grad_ext[count:count + peers * slots].astype(jnp.bfloat16))
            returning = returning.astype(jnp.float32).reshape(peers, slots, edge, edge, edge * width)
            grads = grads.at[device, :count].add(grad_ext[:count])
            grads = grads.at[owners, chosen].add(returning)
            return ((grads, conv_acc + conv_part, down_acc + down_part), output.reshape(count, half, half, half * CO))
        start = (jnp.zeros((peers, count + 1, edge, edge, edge * width), jnp.float32), conv_total, down_total)
        (grads, conv_total, down_total), output = lax.scan(device_step, start, jnp.arange(peers).astype(jnp.int32))
        grads = grads[:, :count]
        outputs.append(output.reshape(NB, half, half, half * CO))
        grad_list.append((grads * keep.astype(jnp.float32)).astype(jnp.bfloat16).reshape(NB, edge, edge, edge * width))
    coarse_out = jnp.stack(outputs, axis=0)
    grad_features = jnp.stack(grad_list, axis=0)
    grad_conv = conv_total * scale
    grad_down = down_total.reshape(8, width, CO) * scale
    return (coarse_out, grad_features, grad_conv, grad_down)
```

```python
import jax
import jax.numpy as jnp
import numpy as np
from jax import lax
from jax.experimental import pallas as pl
from jax.experimental.pallas import tpu as pltpu
from jax.sharding import PartitionSpec as P

F32, BF16 = jnp.float32, jnp.bfloat16
BD = 6
EDGE = 8
HALF = 4
ROWS = EDGE * EDGE
LANES = 512
SHELL = 176
PADR = 112
PADL = 640
EXT = 61
EMPTY = 60
SIDE = 4
GROUP = 9 * 128
VMEM = 58 * 2**20

X_LO, X_HI, Y_LO, Y_HI, Z_AT = 0, 32, 64, 96, 128

PLANE = [(a, b) for a in (-1, 0, 1) for b in (-1, 0, 1) if (a, b) != (0, 0)]


def slots_of(a, b, c):
    return 2 if abs(a) + abs(b) + abs(c) == 1 else 1


def plane_items(a, b):
    own = [(a, b, 0, s) for s in range(slots_of(a, b, 0))]
    return own + [(a, b, -1, 0), (a, b, 1, 0)]


def place(a, b, c):
    return 9 * (a + 1) + 3 * (b + 1) + c + 1


def region(d):
    q = d // 16
    return (q % 2) * 2 + q // 2, (d // 4) % 4, d % 4


def shift_pairs(count, a, b, c):
    where = {region(d): d for d in range(count)}
    pairs = []
    for d in range(count):
        r = region(d)
        to = (r[0] + a, r[1] + b, r[2] + c)
        if to in where:
            pairs.append((d, where[to]))
    return pairs


def pad_row(x, y):
    if 1 <= y <= 8:
        return x * 8 + y - 1
    base = 80 if y == 0 else 96
    return base + (x - 1 if 1 <= x <= 8 else (8 if x == 0 else 9))


def selections():
    sel = np.zeros((9, 4, 16, PADR), np.float32)
    for dx in range(3):
        for dy in range(3):
            for ox in range(2):
                for oy in range(2):
                    for hx in range(4):
                        for hy in range(4):
                            row = pad_row(2 * hx + ox + dx, 2 * hy + oy + dy)
                            sel[dx * 3 + dy, ox * 2 + oy, hx * 4 + hy, row] = 1
    sel = sel.reshape(9, ROWS, PADR)
    return sel.reshape(9 * ROWS, PADR), sel.transpose(0, 2, 1).reshape(9 * PADR, ROWS)


def dot(a, b, ca=1, cb=0):
    return lax.dot_general(a, b, (((ca,), (cb,)), ((), ())), preferred_element_type=F32)


def iota(shape, dim):
    return lax.broadcasted_iota(jnp.int32, shape, dim)


def spread_mask(voxels, width):
    hit = iota((8, LANES), 1) // width == iota((8, LANES), 0) // (width // 64)
    return dot(voxels, hit.astype(F32).astype(BF16))


def low_half(shape):
    return iota(shape, len(shape) - 1) < 64


def row_is(row):
    return iota((8, 128), 0) == row


def choice(me_ref, send_ref, a, b, c, s):
    me = me_ref[0]
    q = me // 16
    r0, r1, r2 = (q % 2) * 2 + q // 2 + a, (me // 4) % 4 + b, me % 4 + c
    inside = (r0 >= 0) & (r0 < SIDE) & (r1 >= 0) & (r1 < SIDE) & (r2 >= 0) & (r2 < SIDE)
    to = ((r0 % 2) * 2 + r0 // 2) * 16 + r1 * 4 + r2
    to = jnp.where(inside, to, 0)
    got = send_ref[to * 2 + s]
    return jnp.clip(jnp.where(inside, got, BD), 0, BD)


def all_items():
    lists = [plane_items(a, b) for a, b in PLANE]
    lists += [[(0, 0, -1, s) for s in range(2)], [(0, 0, 1, s) for s in range(2)]]
    return lists


def pack_kernel(me_ref, send_ref, feat_ref, vox_ref, masked_ref, own_ref, *rest):
    outs, held = rest[:10], rest[10]
    pick = iota((16, ROWS), 1) == (iota((16, ROWS), 0) % 8) * 8 + (iota((16, ROWS), 0) // 8) * 7
    pick = pick.astype(F32).astype(BF16)
    for b in range(BD):
        keep = spread_mask(vox_ref[b * ROWS : (b + 1) * ROWS, :], 64)
        m = feat_ref[b].astype(F32) * keep
        mb = m.astype(BF16)
        masked_ref[b] = mb
        ys = dot(pick, mb)
        tiles = []
        for block in (m[0:8], m[56:64], ys[0:8], ys[8:16]):
            tiles += [block[:, 128 * q : 128 * (q + 1)] for q in range(4)]
        both = jnp.where(low_half((ROWS, 128)), m[:, 0:128], m[:, 384:512])
        tiles.append(both[8:56])
        shell = jnp.concatenate(tiles, axis=0).astype(BF16)
        own_ref[b] = shell
        held[b] = shell
    held[BD] = jnp.zeros((SHELL, 128), BF16)
    for out, items in zip(outs, all_items()):
        for k, item in enumerate(items):
            out[k] = held[choice(me_ref, send_ref, *item)]


def brick_blocks():
    groups = []
    for x, y in ((0, 1), (2, 1), (1, 0), (1, 2)):
        if y == 1:
            first, at = (0, X_HI) if x == 0 else (72, X_LO)
        else:
            first, at = (80, Y_HI) if y == 0 else (96, Y_LO)
        groups.append((first, 9 * x + 3 * y, at))
    return groups


def silu_slope(value, sig):
    return sig * (1.0 + value * (1.0 - sig))


def main_kernel(
    idx_ref, own_ref, masked_ref, voxp_ref, cot_ref, sel_ref, selt_ref, wf_ref, wb_ref, down_ref, *rest
):
    recv = rest[:10]
    coarse_ref, center_ref, gown_ref, sums_ref = rest[10:14]
    outs = rest[14:24]
    ext, gext, pad, cols, slope, kids, grads, gcols, gpad = rest[24:]
    low8 = low_half((8, 128))

    for b in range(BD):
        ext[b] = own_ref[b].astype(F32)
    ext[EMPTY] = jnp.zeros((SHELL, 128), F32)
    for (a, b), ref in zip(PLANE, recv):
        for s in range(slots_of(a, b, 0)):
            ext[BD + 2 * place(-a, -b, 0) + s] = ref[s].astype(F32)
    for c, ref in zip((-1, 1), recv[8:]):
        for s in range(2):
            ext[BD + 2 * place(0, 0, -c) + s] = ref[s].astype(F32)
        for k, (a, b) in enumerate(PLANE):
            ext[BD + 2 * place(-a, -b, -c)] = ref[2 + k].astype(F32)
    gext[...] = jnp.zeros_like(gext)

    @pl.loop(0, BD)
    def _(b):
        base = b * 27

        def src(t, row, size):
            return ext[idx_ref[base + t], row : row + size, :]

        for first, t, at in brick_blocks():
            for q in range(4):
                pad[first : first + 8, 128 * q : 128 * (q + 1)] = src(t + 1, at + 8 * q, 8)
            pad[first : first + 8, 512:640] = jnp.where(low8, src(t + 2, at, 8), src(t, at + 24, 8))
        pad[8:72, 0:512] = masked_ref[b].astype(F32)
        for x in range(8):
            hi_at, lo_at = (X_LO, X_LO + 24) if x == 0 else (X_HI, X_HI + 24) if x == 7 else (Z_AT + 8 * x - 8,) * 2
            pad[8 + 8 * x : 16 + 8 * x, 512:640] = jnp.where(low8, src(14, hi_at, 8), src(12, lo_at, 8))
        for y in (0, 2):
            first = 88 if y == 0 else 104
            row = 7 if y == 0 else 0
            for q in range(5):
                lines = []
                for x in (0, 2):
                    t = 9 * x + 3 * y
                    at = (X_HI if x == 0 else X_LO) + row
                    if q < 4:
                        line = src(t + 1, at + 8 * q, 1)
                    else:
                        line = jnp.where(low_half((1, 128)), src(t + 2, at, 1), src(t, at + 24, 1))
                    lines.append(jnp.broadcast_to(line, (8, 128)))
                pad[first : first + 8, 128 * q : 128 * (q + 1)] = jnp.where(
                    row_is(0), lines[0], jnp.where(row_is(1), lines[1], 0.0)
                )
        turned = pltpu.roll(pad[...], 64, 1).astype(BF16)
        picked = dot(sel_ref[...], turned).astype(BF16)
        for t in range(9):
            for q in range(4):
                rows = picked[t * 64 + q * 16 : t * 64 + q * 16 + 16]
                to = pl.ds(pl.multiple_of(q * 96 + b * 16, 16), 16)
                for k in range(5):
                    cols[to, k * GROUP + t * 128 : k * GROUP + (t + 1) * 128] = rows[:, k * 128 : (k + 1) * 128]

    voxp = voxp_ref[...]
    keep = spread_mask(voxp, 64)
    for p in range(4):
        pre = dot(cols[:, GROUP * p : GROUP * (p + 2)], wf_ref[...])
        kept = keep[:, 128 * p : 128 * (p + 1)]
        pre = pre * kept
        sig = jax.nn.sigmoid(pre)
        slope[:, 128 * p : 128 * (p + 1)] = silu_slope(pre, sig) * kept
        hidden = (pre * sig).astype(BF16)
        for q in range(4):
            kids[p * 96 : (p + 1) * 96, q * 128 : (q + 1) * 128] = hidden[q * 96 : (q + 1) * 96]
    v32 = voxp.astype(F32)
    number = v32[0:96] + v32[96:192] + v32[192:288] + v32[288:384]
    active = (spread_mask(number.astype(BF16), 128) > 0.5).astype(F32)
    pre_out = dot(kids[...], down_ref[...])
    sig = jax.nn.sigmoid(pre_out)
    value = pre_out * sig
    bend = silu_slope(pre_out, sig)
    pieces, parts = [], []
    for p in range(4):
        rows, lanes = slice(96 * p, 96 * (p + 1)), slice(128 * p, 128 * (p + 1))
        pieces.append((value[rows] * active[:, lanes]).astype(BF16))
        parts.append((cot_ref[:, lanes].astype(F32) * active[:, lanes] * bend[rows]).astype(BF16))
    coarse_ref[...] = jnp.concatenate(pieces, axis=1)
    grad_pre = jnp.concatenate(parts, axis=0)

    back = dot(grad_pre, down_ref[...], 1, 1)
    for p in range(4):
        for q in range(4):
            rows, lanes = slice(96 * q, 96 * (q + 1)), slice(128 * p, 128 * (p + 1))
            part = back[96 * p : 96 * (p + 1), 128 * q : 128 * (q + 1)]
            grads[rows, lanes] = (part * slope[rows, lanes]).astype(BF16)

    down_sum = dot(grad_pre, kids[...], 0, 0)
    for q in range(4):
        sums_ref[896 + 128 * q : 1024 + 128 * q, :] = down_sum[:, 128 * q : 128 * (q + 1)]
    total = None
    for p in range(4):
        term = dot(grads[:, 128 * p : 128 * (p + 1)], cols[:, GROUP * p : GROUP * (p + 2)], 0, 0)
        total = term if total is None else total + term
    third = []
    low64 = low_half((64, 128))
    for t in range(9):
        first = total[:, t * 128 : (t + 1) * 128]
        later = total[:, GROUP + t * 128 : GROUP + (t + 1) * 128]
        mixed = pltpu.roll(jnp.where(low64, later[64:], first[64:]), 64, 1)
        sums_ref[64 * t : 64 * (t + 1), :] = first[:64] + mixed
        third.append(later[:64] + pltpu.roll(later[64:], 64, 1))
    third.append(jnp.zeros((64, 128), F32))
    for m in range(5):
        sums_ref[576 + 64 * m : 640 + 64 * m, :] = jnp.where(
            low64, third[2 * m], pltpu.roll(third[2 * m + 1], 64, 1)
        )

    @pl.loop(0, BD)
    def _(b):
        mine = jnp.concatenate(
            [grads[pl.ds(pl.multiple_of(q * 96 + b * 16, 16), 16), :] for q in range(4)], axis=0
        )
        placed = dot(selt_ref[...], mine).astype(BF16)
        to = pl.ds(pl.multiple_of(b * PADR, 16), PADR)
        for t in range(9):
            for k in range(4):
                gcols[to, k * GROUP + t * 128 : k * GROUP + (t + 1) * 128] = placed[
                    t * PADR : (t + 1) * PADR, k * 128 : (k + 1) * 128
                ]

    for j in range(5):
        lo, hi = max(j - 1, 0), min(j + 1, 4)
        w_lo = GROUP if j == 0 else 0
        w_hi = GROUP if j == 4 else 2 * GROUP
        gpad[:, 128 * j : 128 * (j + 1)] = dot(gcols[:, GROUP * lo : GROUP * hi], wb_ref[w_lo:w_hi, :])

    @pl.loop(0, BD)
    def _(b):
        base = b * 27
        g = pltpu.roll(gpad[pl.ds(pl.multiple_of(b * PADR, 8), PADR), :], PADL - 64, 1)
        center_ref[b] = g[8:72, 0:512]

        def add(t, row, data):
            at = idx_ref[base + t]
            gext[at, row : row + data.shape[0], :] = gext[at, row : row + data.shape[0], :] + data

        for first, t, at in brick_blocks():
            for q in range(4):
                add(t + 1, at + 8 * q, g[first : first + 8, 128 * q : 128 * (q + 1)])
            rim = g[first : first + 8, 512:640]
            add(t + 2, at, jnp.where(low8, rim, 0.0))
            add(t, at + 24, jnp.where(low8, 0.0, rim))
        for x in range(8):
            hi_at, lo_at = (X_LO, X_LO + 24) if x == 0 else (X_HI, X_HI + 24) if x == 7 else (Z_AT + 8 * x - 8,) * 2
            rim = g[8 + 8 * x : 16 + 8 * x, 512:640]
            add(14, hi_at, jnp.where(low8, rim, 0.0))
            add(12, lo_at, jnp.where(low8, 0.0, rim))
        for y in (0, 2):
            first = 88 if y == 0 else 104
            row = 7 if y == 0 else 0
            for n, x in enumerate((0, 2)):
                t = 9 * x + 3 * y
                at = X_HI if x == 0 else X_LO
                for q in range(5):
                    line = jnp.broadcast_to(g[first + n : first + n + 1, 128 * q : 128 * (q + 1)], (8, 128))
                    line = jnp.where(row_is(row), line, 0.0)
                    if q < 4:
                        add(t + 1, at + 8 * q, line)
                    else:
                        add(t + 2, at, jnp.where(low8, line, 0.0))
                        add(t, at + 24, jnp.where(low8, 0.0, line))

    for b in range(BD):
        gown_ref[b] = gext[b]
    for out, items in zip(outs, all_items()):
        for k, (a, b, c, s) in enumerate(items):
            out[k] = gext[BD + 2 * place(a, b, c) + s].astype(BF16)


def last_kernel(me_ref, send_ref, vox_ref, center_ref, gown_ref, *rest):
    recv, out_ref, acc = rest[:10], rest[10], rest[11]
    for b in range(BD):
        acc[b] = gown_ref[b]
    acc[BD] = jnp.zeros((SHELL, 128), F32)

    def add(data, *item):
        at = choice(me_ref, send_ref, *item)
        acc[at] = acc[at] + data.astype(F32)

    for (a, b), ref in zip(PLANE, recv):
        for s in range(slots_of(a, b, 0)):
            add(ref[s], -a, -b, 0, s)
    for c, ref in zip((-1, 1), recv[8:]):
        for s in range(2):
            add(ref[s], 0, 0, -c, s)
        for k, (a, b) in enumerate(PLANE):
            add(ref[2 + k], -a, -b, -c, 0)
    low8 = low_half((8, 128))
    for b in range(BD):
        keep = spread_mask(vox_ref[b * ROWS : (b + 1) * ROWS, :], 64)
        lines = []
        for x in range(8):
            blocks = []
            for q in range(4):
                v = center_ref[b, 8 * x : 8 * x + 8, 128 * q : 128 * (q + 1)]
                y_lo = acc[b, Y_LO + 8 * q + x : Y_LO + 8 * q + x + 1, :]
                y_hi = acc[b, Y_HI + 8 * q + x : Y_HI + 8 * q + x + 1, :]
                v = v + jnp.where(row_is(0), jnp.broadcast_to(y_lo, (8, 128)), 0.0)
                v = v + jnp.where(row_is(7), jnp.broadcast_to(y_hi, (8, 128)), 0.0)
                if x == 0:
                    v = v + acc[b, X_LO + 8 * q : X_LO + 8 * q + 8, :]
                if x == 7:
                    v = v + acc[b, X_HI + 8 * q : X_HI + 8 * q + 8, :]
                if 1 <= x <= 6 and q in (0, 3):
                    z = acc[b, Z_AT + 8 * x - 8 : Z_AT + 8 * x, :]
                    v = v + (jnp.where(low8, z, 0.0) if q == 0 else jnp.where(low8, 0.0, z))
                blocks.append(v)
            lines.append(jnp.concatenate(blocks, axis=1))
        dense = jnp.concatenate(lines, axis=0)
        out_ref[b] = (dense * keep).astype(BF16)


def finish_kernel(scale, place_ref, near_ref, far_ref, conv_ref, down_ref, held):
    x, core = place_ref[0], place_ref[1]
    for k in range(4):
        at = jnp.bitwise_xor(x, k)
        held[core * 4 + at] = near_ref[k].astype(F32) * scale
        held[(1 - core) * 4 + at] = far_ref[k].astype(F32) * scale
    full = jnp.concatenate([held[k] for k in range(8)], axis=0)
    for t in range(9):
        turned = full[64 * t : 64 * (t + 1)].T
        conv_ref[3 * t] = turned[:64]
        conv_ref[3 * t + 1] = turned[64:]
    for m in range(5):
        turned = full[576 + 64 * m : 640 + 64 * m].T
        conv_ref[6 * m + 2] = turned[:64]
        if m < 4:
            conv_ref[6 * m + 5] = turned[64:]
    for q in range(4):
        turned = full[896 + 128 * q : 1024 + 128 * q].T
        down_ref[2 * q] = turned[:64]
        down_ref[2 * q + 1] = turned[64:]


def call(kernel, outs, args, smem, scratch=(), flops=0):
    spec_s = pl.BlockSpec(memory_space=pltpu.SMEM)
    spec_v = pl.BlockSpec(memory_space=pltpu.VMEM)
    moved = sum(int(np.prod(v.shape)) * v.dtype.itemsize for v in (*args, *outs))
    return pl.pallas_call(
        kernel,
        out_shape=outs,
        in_specs=[spec_s] * smem + [spec_v] * (len(args) - smem),
        out_specs=[spec_v] * len(outs),
        scratch_shapes=list(scratch),
        compiler_params=pltpu.CompilerParams(vmem_limit_bytes=VMEM),
        cost_estimate=pl.CostEstimate(flops=flops, bytes_accessed=moved, transcendentals=0),
    )(*args)


def exchange(parts, peers):
    got = [lax.ppermute(v, "spatial", shift_pairs(peers, a, b, 0)) for (a, b), v in zip(PLANE, parts)]
    along = []
    for n, c in enumerate((-1, 1)):
        pieces = [parts[8 + n]]
        for v in got:
            at = v.shape[0] - 2 + n
            pieces.append(v[at : at + 1])
        along.append(lax.ppermute(jnp.concatenate(pieces, axis=0), "spatial", shift_pairs(peers, 0, 0, c)))
    return got + along


def pair_weights(taps, width):
    zero = jnp.zeros((3, 3, 1, width, width), taps.dtype)
    first = jnp.concatenate([taps, zero], axis=2)
    second = jnp.concatenate([zero, taps], axis=2)
    both = jnp.stack([first, second], axis=4).reshape(9, 2, 2 * width, 2 * width)
    return both.transpose(1, 0, 2, 3).reshape(2 * GROUP, 2 * width)


def reduce_sums(sums, me, x, peers):
    core = me % 2
    halves = sums.reshape(2, 4, SHELL, 128)
    near = lax.dynamic_index_in_dim(halves, core, 0, keepdims=False)
    far = lax.dynamic_index_in_dim(halves, 1 - core, 0, keepdims=False)

    def swap(v, bit):
        return lax.ppermute(v, "spatial", [(d, d ^ bit) for d in range(peers)])

    def swap_x(v, bit):
        return lax.ppermute(v, "dp", [(d, d ^ bit) for d in range(4)])

    mine = near + swap(far.astype(BF16), 1).astype(F32)
    small = mine.astype(BF16)
    v = lax.dynamic_index_in_dim(mine, x, 0, keepdims=False)
    for k in (1, 2, 3):
        part = lax.dynamic_index_in_dim(small, jnp.bitwise_xor(x, k), 0, keepdims=False)
        v = v + swap_x(part, k).astype(F32)

    def pairs(v, bits):
        w = v.astype(BF16)
        got = [w.astype(F32)] + [swap(w, bit).astype(F32) for bit in bits]
        while len(got) > 1:
            got = [got[i] + got[i + 1] for i in range(0, len(got), 2)]
        return got[0]

    v = pairs(v, (16, 32, 48))
    v = pairs(v, (2,))
    v = pairs(v, (4, 8, 12))
    w = v.astype(BF16)
    near = jnp.stack([w] + [swap_x(w, k) for k in (1, 2, 3)])
    return near, swap(near, 1)


def shards(features, masks, rulebook, send_lists, conv_weight, down_weight, cotangent):
    peers = lax.axis_size("spatial")
    me = lax.axis_index("spatial").astype(jnp.int32)
    x = lax.axis_index("dp").astype(jnp.int32)
    me_s = me.reshape(1)
    sends = send_lists.reshape(peers * 2)
    feat = features.reshape(BD, ROWS, LANES)
    cot = cotangent.reshape(BD * 16, LANES)
    vox = masks.reshape(BD * ROWS, 8).astype(BF16)
    voxp = vox.reshape(BD, 4, 2, 4, 2, 8).transpose(2, 4, 0, 1, 3, 5).reshape(BD * ROWS, 8)

    brick = jax.ShapeDtypeStruct((BD, ROWS, LANES), BF16)
    parts = [jax.ShapeDtypeStruct((len(items), SHELL, 128), BF16) for items in all_items()]
    held = pltpu.VMEM((BD + 1, SHELL, 128), BF16)
    own_shape = jax.ShapeDtypeStruct((BD, SHELL, 128), BF16)
    masked, own, *sent = call(pack_kernel, [brick, own_shape, *parts], [me_s, sends, feat, vox], 2, [held])
    recv = exchange(sent, peers)

    entry = rulebook.reshape(BD * 27)
    other = jnp.clip(entry - BD, 0, 2 * peers - 1)
    p = other // 2
    apart = []
    for theirs, ours in zip(region(p), region(me)):
        apart.append(jnp.clip(theirs - ours, -1, 1))
    there = BD + 2 * place(*apart) + other % 2
    idx = jnp.where(entry < BD, entry, jnp.where(entry >= BD + 2 * peers, EMPTY, there)).astype(jnp.int32)
    idx = jnp.clip(idx, 0, EMPTY)

    taps = conv_weight.reshape(3, 3, 3, 64, 64)
    wf = pair_weights(taps, 64)
    wb = pair_weights(taps[:, :, ::-1].transpose(0, 1, 2, 4, 3), 64)
    down = down_weight.reshape(512, 128)
    sel, selt = (jnp.asarray(v, BF16) for v in selections())
    outs = [
        jax.ShapeDtypeStruct((BD * 16, LANES), BF16),
        jax.ShapeDtypeStruct((BD, ROWS, LANES), F32),
        jax.ShapeDtypeStruct((BD, SHELL, 128), F32),
        jax.ShapeDtypeStruct((8 * SHELL, 128), F32),
        *parts,
    ]
    scratch = [
        pltpu.VMEM((EXT, SHELL, 128), F32),
        pltpu.VMEM((EXT, SHELL, 128), F32),
        pltpu.VMEM((PADR, PADL), F32),
        pltpu.VMEM((BD * ROWS, 5 * GROUP), BF16),
        pltpu.VMEM((BD * ROWS, LANES), F32),
        pltpu.VMEM((BD * ROWS, LANES), BF16),
        pltpu.VMEM((BD * ROWS, LANES), BF16),
        pltpu.VMEM((BD * PADR, 4 * GROUP), BF16),
        pltpu.VMEM((BD * PADR, PADL), F32),
    ]
    coarse, center, gown, sums, *back = call(
        main_kernel, outs, [idx, own, masked, voxp, cot, sel, selt, wf, wb, down, *recv], 1, scratch, 10**10
    )
    came = exchange(back, peers)
    near, far = reduce_sums(sums, me, x, peers)
    [grad] = call(
        last_kernel,
        [brick],
        [me_s, sends, vox, center, gown, *came],
        2,
        [pltpu.VMEM((BD + 1, SHELL, 128), F32)],
    )
    scale = float(lax.axis_size("dp") * peers * BD * EDGE**3) ** (-0.5)
    spot = jnp.stack([x, me % 2])
    conv_sum, down_sum = call(
        lambda *refs: finish_kernel(scale, *refs),
        [jax.ShapeDtypeStruct((27, 64, 64), F32), jax.ShapeDtypeStruct((8, 64, 128), F32)],
        [spot, near, far],
        1,
        [pltpu.VMEM((8, SHELL, 128), F32)],
    )
    return (
        coarse.reshape(cotangent.shape),
        grad.reshape(features.shape),
        conv_sum,
        down_sum,
    )


def solution(mesh):
    placed = (
        P("dp", "spatial", None, None, None),
        P("dp", "spatial", None),
        P("dp", "spatial", None),
        P("dp", "spatial", None, None),
        P(),
        P(),
        P("dp", "spatial", None, None, None),
    )
    return jax.shard_map(
        shards,
        mesh=mesh,
        in_specs=placed,
        out_specs=(
            P("dp", "spatial", None, None, None),
            P("dp", "spatial", None, None, None),
            P(),
            P(),
        ),
        check_vma=False,
    )
```

```python
import jax
import jax.numpy as jnp
import numpy as np
from jax import lax
from jax.experimental import pallas as pl
from jax.experimental.pallas import tpu as pltpu
from jax.sharding import PartitionSpec as P

F32, BF16 = jnp.float32, jnp.bfloat16
BD = 6
EDGE = 8
HALF = 4
ROWS = EDGE * EDGE
LANES = 512
SHELL = 176
PADR = 112
PADL = 640
EXT = 61
EMPTY = 60
SIDE = 4
GROUP = 9 * 128
VMEM = 58 * 2**20

X_LO, X_HI, Y_LO, Y_HI, Z_AT = 0, 32, 64, 96, 128

PLANE = [(1, 1), (1, 0), (1, -1), (0, 1), (0, -1), (-1, 1), (-1, 0), (-1, -1)]


def slots_of(a, b, c):
    return 2 if abs(a) + abs(b) + abs(c) == 1 else 1


def plane_items(u, w, by):
    a, b, near = u * by[0], w * by[1], by[2]
    own = [(a, b, 0, s) for s in range(slots_of(u, w, 0))]
    return own + [(a, b, near, 0), (a, b, -near, 0)]


def place(a, b, c):
    return 9 * (a + 1) + 3 * (b + 1) + c + 1


def region(d):
    q = d // 16
    return (q % 2) * 2 + q // 2, (d // 4) % 4, d % 4


def steps(d):
    return tuple(1 - 2 * (r % 2) for r in region(d))


def swap_pairs(count, u, w):
    where = {region(d): d for d in range(count)}
    pairs = []
    for d in range(count):
        r, by = region(d), steps(d)
        to = (r[0] + u * by[0], r[1] + w * by[1], r[2])
        if to in where:
            pairs.append((d, where[to]))
    return pairs


def pad_row(x, y):
    if 1 <= y <= 8:
        return x * 8 + y - 1
    base = 80 if y == 0 else 96
    return base + (x - 1 if 1 <= x <= 8 else (8 if x == 0 else 9))


def selections():
    sel = np.zeros((9, 4, 16, PADR), np.float32)
    for dx in range(3):
        for dy in range(3):
            for ox in range(2):
                for oy in range(2):
                    for hx in range(4):
                        for hy in range(4):
                            row = pad_row(2 * hx + ox + dx, 2 * hy + oy + dy)
                            sel[dx * 3 + dy, ox * 2 + oy, hx * 4 + hy, row] = 1
    sel = sel.reshape(9, ROWS, PADR)
    return sel.reshape(9 * ROWS, PADR), sel.transpose(0, 2, 1).reshape(9 * PADR, ROWS)


def dot(a, b, ca=1, cb=0):
    return lax.dot_general(a, b, (((ca,), (cb,)), ((), ())), preferred_element_type=F32)


def iota(shape, dim):
    return lax.broadcasted_iota(jnp.int32, shape, dim)


def spread_mask(voxels, width):
    hit = iota((128, LANES), 1) // width == iota((128, LANES), 0) // (width // 64)
    return dot(voxels, hit.astype(F32).astype(BF16))


def voxel_rows(mask_ref, permuted):
    deep = (iota((LANES, 128), 0) % 8 == iota((LANES, 128), 1)).astype(F32).astype(BF16)
    masks = [mask_ref[b].astype(F32) for b in range(BD)]
    pieces = []
    if permuted:
        row, lane = iota((16, LANES), 0), iota((16, LANES), 1) // 8
        for q in range(4):
            mine = (2 * (row // 4) + q // 2) * 8 + 2 * (row % 4) + q % 2 == lane
            for b in range(BD):
                pieces.append(jnp.where(mine, jnp.broadcast_to(masks[b], (16, LANES)), 0.0))
    else:
        mine = iota((ROWS, LANES), 0) == iota((ROWS, LANES), 1) // 8
        for b in range(BD):
            pieces.append(jnp.where(mine, jnp.broadcast_to(masks[b], (ROWS, LANES)), 0.0))
    return dot(jnp.concatenate(pieces, axis=0).astype(BF16), deep).astype(BF16)


def low_half(shape):
    return iota(shape, len(shape) - 1) < 64


def row_is(row):
    return iota((8, 128), 0) == row


def choice(me_ref, send_ref, a, b, c, s):
    me = me_ref[0]
    q = me // 16
    r0, r1, r2 = (q % 2) * 2 + q // 2 + a, (me // 4) % 4 + b, me % 4 + c
    inside = (r0 >= 0) & (r0 < SIDE) & (r1 >= 0) & (r1 < SIDE) & (r2 >= 0) & (r2 < SIDE)
    to = ((r0 % 2) * 2 + r0 // 2) * 16 + r1 * 4 + r2
    to = jnp.where(inside, to, 0)
    got = send_ref[s, to]
    return jnp.clip(jnp.where(inside, got, BD), 0, BD)


def all_items(by=(1, 1, 1)):
    lists = [plane_items(u, w, by) for u, w in PLANE]
    lists += [[(0, 0, by[2], s) for s in range(2)], [(0, 0, -by[2], s) for s in range(2)]]
    return lists


def received_items(by):
    lists = [[(u * by[0], w * by[1], 0, s) for s in range(slots_of(u, w, 0))] for u, w in PLANE]
    for c in (by[2], -by[2]):
        lists.append([(0, 0, c, s) for s in range(2)] + [(u * by[0], w * by[1], c, 0) for u, w in PLANE])
    return lists


def pack_kernel(me_ref, send_ref, feat_ref, mask_ref, masked_ref, own_ref, *rest):
    outs, held = rest[:10], rest[10]
    pick = iota((16, ROWS), 1) == (iota((16, ROWS), 0) % 8) * 8 + (iota((16, ROWS), 0) // 8) * 7
    pick = pick.astype(F32).astype(BF16)
    voxels = voxel_rows(mask_ref, False)
    for b in range(BD):
        keep = spread_mask(voxels[b * ROWS : (b + 1) * ROWS], 64)
        m = feat_ref[b].astype(F32) * keep
        mb = m.astype(BF16)
        masked_ref[b] = mb
        ys = dot(pick, mb)
        tiles = []
        for block in (m[0:8], m[56:64], ys[0:8], ys[8:16]):
            tiles += [block[:, 128 * q : 128 * (q + 1)] for q in range(4)]
        both = jnp.where(low_half((ROWS, 128)), m[:, 0:128], m[:, 384:512])
        tiles.append(both[8:56])
        shell = jnp.concatenate(tiles, axis=0).astype(BF16)
        own_ref[b] = shell
        held[b] = shell
    held[BD] = jnp.zeros((SHELL, 128), BF16)
    for out, items in zip(outs, all_items(steps(me_ref[0]))):
        for k, item in enumerate(items):
            out[k] = held[choice(me_ref, send_ref, *item)]


def brick_blocks():
    groups = []
    for x, y in ((0, 1), (2, 1), (1, 0), (1, 2)):
        if y == 1:
            first, at = (0, X_HI) if x == 0 else (72, X_LO)
        else:
            first, at = (80, Y_HI) if y == 0 else (96, Y_LO)
        groups.append((first, 9 * x + 3 * y, at))
    return groups


def silu_slope(value, sig):
    return sig * (1.0 + value * (1.0 - sig))


def main_kernel(
    idx_ref, me_ref, own_ref, masked_ref, mask_ref, cot_ref, sel_ref, selt_ref, wf_ref, wb_ref, down_ref, *rest
):
    recv = rest[:10]
    coarse_ref, center_ref, gown_ref, sums_ref = rest[10:14]
    outs = rest[14:24]
    ext, gext, pad, cols, slope, kids, grads, gcols, gpad = rest[24:]
    low8 = low_half((8, 128))

    for b in range(BD):
        ext[b] = own_ref[b].astype(F32)
    ext[EMPTY] = jnp.zeros((SHELL, 128), F32)
    by = steps(me_ref[0])
    for ref, items in zip(recv, received_items(by)):
        for k, (a, b, c, s) in enumerate(items):
            ext[BD + 2 * place(a, b, c) + s] = ref[k].astype(F32)
    gext[...] = jnp.zeros_like(gext)

    @pl.loop(0, BD)
    def _(b):
        base = b * 27

        def src(t, row, size):
            return ext[idx_ref[base + t], row : row + size, :]

        for first, t, at in brick_blocks():
            for q in range(4):
                pad[first : first + 8, 128 * q : 128 * (q + 1)] = src(t + 1, at + 8 * q, 8)
            pad[first : first + 8, 512:640] = jnp.where(low8, src(t + 2, at, 8), src(t, at + 24, 8))
        pad[8:72, 0:512] = masked_ref[b].astype(F32)
        for x in range(8):
            hi_at, lo_at = (X_LO, X_LO + 24) if x == 0 else (X_HI, X_HI + 24) if x == 7 else (Z_AT + 8 * x - 8,) * 2
            pad[8 + 8 * x : 16 + 8 * x, 512:640] = jnp.where(low8, src(14, hi_at, 8), src(12, lo_at, 8))
        for y in (0, 2):
            first = 88 if y == 0 else 104
            row = 7 if y == 0 else 0
            for q in range(5):
                lines = []
                for x in (0, 2):
                    t = 9 * x + 3 * y
                    at = (X_HI if x == 0 else X_LO) + row
                    if q < 4:
                        line = src(t + 1, at + 8 * q, 1)
                    else:
                        line = jnp.where(low_half((1, 128)), src(t + 2, at, 1), src(t, at + 24, 1))
                    lines.append(jnp.broadcast_to(line, (8, 128)))
                pad[first : first + 8, 128 * q : 128 * (q + 1)] = jnp.where(
                    row_is(0), lines[0], jnp.where(row_is(1), lines[1], 0.0)
                )
        turned = pltpu.roll(pad[...], 64, 1).astype(BF16)
        picked = dot(sel_ref[...], turned).astype(BF16)
        for t in range(9):
            for q in range(4):
                rows = picked[t * 64 + q * 16 : t * 64 + q * 16 + 16]
                to = pl.ds(pl.multiple_of(q * 96 + b * 16, 16), 16)
                for k in range(5):
                    cols[to, k * GROUP + t * 128 : k * GROUP + (t + 1) * 128] = rows[:, k * 128 : (k + 1) * 128]

    voxp = voxel_rows(mask_ref, True)
    keep = spread_mask(voxp, 64)
    for p in range(4):
        pre = dot(cols[:, GROUP * p : GROUP * (p + 2)], wf_ref[...])
        kept = keep[:, 128 * p : 128 * (p + 1)]
        pre = pre * kept
        sig = jax.nn.sigmoid(pre)
        slope[:, 128 * p : 128 * (p + 1)] = silu_slope(pre, sig) * kept
        hidden = (pre * sig).astype(BF16)
        for q in range(4):
            kids[p * 96 : (p + 1) * 96, q * 128 : (q + 1) * 128] = hidden[q * 96 : (q + 1) * 96]
    v32 = voxp.astype(F32)
    number = v32[0:96] + v32[96:192] + v32[192:288] + v32[288:384]
    active = (spread_mask(number.astype(BF16), 128) > 0.5).astype(F32)
    pre_out = dot(kids[...], down_ref[...])
    sig = jax.nn.sigmoid(pre_out)
    value = pre_out * sig
    bend = silu_slope(pre_out, sig)
    pieces, parts = [], []
    for p in range(4):
        rows, lanes = slice(96 * p, 96 * (p + 1)), slice(128 * p, 128 * (p + 1))
        pieces.append(value[rows] * active[:, lanes])
        parts.append((cot_ref[:, lanes].astype(F32) * active[:, lanes] * bend[rows]).astype(BF16))
    coarse = jnp.concatenate(pieces, axis=1)
    for k in range(BD * HALF):
        coarse_ref[k] = coarse[HALF * k : HALF * (k + 1)].astype(BF16)
    grad_pre = jnp.concatenate(parts, axis=0)

    back = dot(grad_pre, down_ref[...], 1, 1)
    for p in range(4):
        for q in range(4):
            rows, lanes = slice(96 * q, 96 * (q + 1)), slice(128 * p, 128 * (p + 1))
            part = back[96 * p : 96 * (p + 1), 128 * q : 128 * (q + 1)]
            grads[rows, lanes] = (part * slope[rows, lanes]).astype(BF16)

    down_sum = dot(grad_pre, kids[...], 0, 0)
    for q in range(4):
        sums_ref[896 + 128 * q : 1024 + 128 * q, :] = down_sum[:, 128 * q : 128 * (q + 1)]
    total = None
    for p in range(4):
        term = dot(grads[:, 128 * p : 128 * (p + 1)], cols[:, GROUP * p : GROUP * (p + 2)], 0, 0)
        total = term if total is None else total + term
    third = []
    low64 = low_half((64, 128))
    for t in range(9):
        first = total[:, t * 128 : (t + 1) * 128]
        later = total[:, GROUP + t * 128 : GROUP + (t + 1) * 128]
        mixed = pltpu.roll(jnp.where(low64, later[64:], first[64:]), 64, 1)
        sums_ref[64 * t : 64 * (t + 1), :] = first[:64] + mixed
        third.append(later[:64] + pltpu.roll(later[64:], 64, 1))
    third.append(jnp.zeros((64, 128), F32))
    for m in range(5):
        sums_ref[576 + 64 * m : 640 + 64 * m, :] = jnp.where(
            low64, third[2 * m], pltpu.roll(third[2 * m + 1], 64, 1)
        )

    @pl.loop(0, BD)
    def _(b):
        mine = jnp.concatenate(
            [grads[pl.ds(pl.multiple_of(q * 96 + b * 16, 16), 16), :] for q in range(4)], axis=0
        )
        placed = dot(selt_ref[...], mine).astype(BF16)
        to = pl.ds(pl.multiple_of(b * PADR, 16), PADR)
        for t in range(9):
            for k in range(4):
                gcols[to, k * GROUP + t * 128 : k * GROUP + (t + 1) * 128] = placed[
                    t * PADR : (t + 1) * PADR, k * 128 : (k + 1) * 128
                ]

    for j in range(5):
        lo, hi = max(j - 1, 0), min(j + 1, 4)
        w_lo = GROUP if j == 0 else 0
        w_hi = GROUP if j == 4 else 2 * GROUP
        gpad[:, 128 * j : 128 * (j + 1)] = dot(gcols[:, GROUP * lo : GROUP * hi], wb_ref[w_lo:w_hi, :])

    @pl.loop(0, BD)
    def _(b):
        base = b * 27
        g = pltpu.roll(gpad[pl.ds(pl.multiple_of(b * PADR, 8), PADR), :], PADL - 64, 1)
        center_ref[b] = g[8:72, 0:512]

        def add(t, row, data):
            at = idx_ref[base + t]
            gext[at, row : row + data.shape[0], :] = gext[at, row : row + data.shape[0], :] + data

        for first, t, at in brick_blocks():
            for q in range(4):
                add(t + 1, at + 8 * q, g[first : first + 8, 128 * q : 128 * (q + 1)])
            rim = g[first : first + 8, 512:640]
            add(t + 2, at, jnp.where(low8, rim, 0.0))
            add(t, at + 24, jnp.where(low8, 0.0, rim))
        for x in range(8):
            hi_at, lo_at = (X_LO, X_LO + 24) if x == 0 else (X_HI, X_HI + 24) if x == 7 else (Z_AT + 8 * x - 8,) * 2
            rim = g[8 + 8 * x : 16 + 8 * x, 512:640]
            add(14, hi_at, jnp.where(low8, rim, 0.0))
            add(12, lo_at, jnp.where(low8, 0.0, rim))
        for y in (0, 2):
            first = 88 if y == 0 else 104
            row = 7 if y == 0 else 0
            for n, x in enumerate((0, 2)):
                t = 9 * x + 3 * y
                at = X_HI if x == 0 else X_LO
                for q in range(5):
                    line = jnp.broadcast_to(g[first + n : first + n + 1, 128 * q : 128 * (q + 1)], (8, 128))
                    line = jnp.where(row_is(row), line, 0.0)
                    if q < 4:
                        add(t + 1, at + 8 * q, line)
                    else:
                        add(t + 2, at, jnp.where(low8, line, 0.0))
                        add(t, at + 24, jnp.where(low8, 0.0, line))

    for b in range(BD):
        gown_ref[b] = gext[b]
    for out, items in zip(outs, all_items(by)):
        for k, (a, b, c, s) in enumerate(items):
            out[k] = gext[BD + 2 * place(a, b, c) + s].astype(BF16)


def last_kernel(me_ref, send_ref, mask_ref, center_ref, gown_ref, *rest):
    recv, out_ref, acc = rest[:10], rest[10], rest[11]
    for b in range(BD):
        acc[b] = gown_ref[b]
    acc[BD] = jnp.zeros((SHELL, 128), F32)

    def add(data, *item):
        at = choice(me_ref, send_ref, *item)
        acc[at] = acc[at] + data.astype(F32)

    for ref, items in zip(recv, received_items(steps(me_ref[0]))):
        for k, item in enumerate(items):
            add(ref[k], *item)
    low8 = low_half((8, 128))
    voxels = voxel_rows(mask_ref, False)
    for b in range(BD):
        keep = spread_mask(voxels[b * ROWS : (b + 1) * ROWS], 64)
        lines = []
        for x in range(8):
            blocks = []
            for q in range(4):
                v = center_ref[b, 8 * x : 8 * x + 8, 128 * q : 128 * (q + 1)]
                y_lo = acc[b, Y_LO + 8 * q + x : Y_LO + 8 * q + x + 1, :]
                y_hi = acc[b, Y_HI + 8 * q + x : Y_HI + 8 * q + x + 1, :]
                v = v + jnp.where(row_is(0), jnp.broadcast_to(y_lo, (8, 128)), 0.0)
                v = v + jnp.where(row_is(7), jnp.broadcast_to(y_hi, (8, 128)), 0.0)
                if x == 0:
                    v = v + acc[b, X_LO + 8 * q : X_LO + 8 * q + 8, :]
                if x == 7:
                    v = v + acc[b, X_HI + 8 * q : X_HI + 8 * q + 8, :]
                if 1 <= x <= 6 and q in (0, 3):
                    z = acc[b, Z_AT + 8 * x - 8 : Z_AT + 8 * x, :]
                    v = v + (jnp.where(low8, z, 0.0) if q == 0 else jnp.where(low8, 0.0, z))
                blocks.append(v)
            lines.append(jnp.concatenate(blocks, axis=1))
        dense = jnp.concatenate(lines, axis=0)
        out_ref[b] = (dense * keep).astype(BF16)


def finish_kernel(scale, place_ref, near_ref, far_ref, conv_ref, down_ref, held):
    x, core = place_ref[0], place_ref[1]
    for k in range(4):
        at = jnp.bitwise_xor(x, k)
        held[core * 4 + at] = near_ref[k].astype(F32) * scale
        held[(1 - core) * 4 + at] = far_ref[k].astype(F32) * scale
    full = jnp.concatenate([held[k] for k in range(8)], axis=0)
    for t in range(9):
        turned = full[64 * t : 64 * (t + 1)].T
        conv_ref[3 * t] = turned[:64]
        conv_ref[3 * t + 1] = turned[64:]
    for m in range(5):
        turned = full[576 + 64 * m : 640 + 64 * m].T
        conv_ref[6 * m + 2] = turned[:64]
        if m < 4:
            conv_ref[6 * m + 5] = turned[64:]
    for q in range(4):
        turned = full[896 + 128 * q : 1024 + 128 * q].T
        down_ref[2 * q] = turned[:64]
        down_ref[2 * q + 1] = turned[64:]


def call(kernel, outs, args, smem, scratch=(), flops=0):
    spec_s = pl.BlockSpec(memory_space=pltpu.SMEM)
    spec_v = pl.BlockSpec(memory_space=pltpu.VMEM)
    moved = sum(int(np.prod(v.shape)) * v.dtype.itemsize for v in (*args, *outs))
    return pl.pallas_call(
        kernel,
        out_shape=outs,
        in_specs=[spec_s] * smem + [spec_v] * (len(args) - smem),
        out_specs=[spec_v] * len(outs),
        scratch_shapes=list(scratch),
        compiler_params=pltpu.CompilerParams(vmem_limit_bytes=VMEM),
        cost_estimate=pl.CostEstimate(flops=flops, bytes_accessed=moved, transcendentals=0),
    )(*args)


def exchange_plane(parts, peers):
    return [lax.ppermute(v, "spatial", swap_pairs(peers, a, b)) for (a, b), v in zip(PLANE, parts)]


def exchange_along(got, parts, peers):
    swaps = [[(d, d ^ 1) for d in range(peers)]]
    swaps += [[(d, d + 1 if d % SIDE == 1 else d - 1) for d in range(peers) if d % SIDE in (1, 2)]]
    along = []
    for n in (1, 0):
        pieces = [parts[8 + n]]
        for v in got:
            at = v.shape[0] - 2 + n
            pieces.append(v[at : at + 1])
        along.append(lax.ppermute(jnp.concatenate(pieces, axis=0), "spatial", swaps[n]))
    return [*got, along[1], along[0]]


def exchange(parts, peers):
    return exchange_along(exchange_plane(parts, peers), parts, peers)


def pair_weights(taps, width):
    zero = jnp.zeros((3, 3, 1, width, width), taps.dtype)
    first = jnp.concatenate([taps, zero], axis=2)
    second = jnp.concatenate([zero, taps], axis=2)
    both = jnp.stack([first, second], axis=4).reshape(9, 2, 2 * width, 2 * width)
    return both.transpose(1, 0, 2, 3).reshape(2 * GROUP, 2 * width)


def after(values, earlier):
    return lax.optimization_barrier((tuple(values), earlier))[0]


def exchange_and_sum(parts, sums, me, x, peers):
    core = me % 2
    got = {}

    def plane(lo, hi, earlier=None):
        keys = PLANE[lo:hi]
        ins = [parts[PLANE.index(k)] for k in keys]
        if earlier is not None:
            ins = after(ins, earlier)
        for k, v in zip(keys, ins):
            got[k] = lax.ppermute(v, "spatial", swap_pairs(peers, *k))

    def swap(v, bit):
        return lax.ppermute(v, "spatial", [(d, d ^ bit) for d in range(peers)])

    def swap_x(v, bit):
        return lax.ppermute(v, "dp", [(d, d ^ bit) for d in range(4)])

    def one_of(v, at):
        return lax.dynamic_index_in_dim(v, at, 0, keepdims=False)

    def pairs(w, bits):
        all_of = [w.astype(F32)] + [swap(w, bit).astype(F32) for bit in bits]
        while len(all_of) > 1:
            all_of = [all_of[i] + all_of[i + 1] for i in range(0, len(all_of), 2)]
        return all_of[0].astype(BF16)

    halves = sums.reshape(2, 4, SHELL, 128)
    plane(0, 4)
    mine = one_of(halves, core) + swap(one_of(halves, 1 - core).astype(BF16), 1).astype(F32)
    small = mine.astype(BF16)
    away = [one_of(small, jnp.bitwise_xor(x, k)) for k in (1, 2, 3)]
    plane(4, 8, tuple(away))
    v = one_of(mine, x)
    for k in (1, 2, 3):
        v = v + swap_x(away[k - 1], k).astype(F32)
    w = v.astype(BF16)
    w = pairs(w, (16, 32, 48))
    w = pairs(w, (2,))
    w = pairs(w, (4, 8, 12))
    near = jnp.stack([w] + [swap_x(w, k) for k in (1, 2, 3)])
    came = exchange_along([got[k] for k in PLANE], parts, peers)
    return came, near, swap(near, 1)


def shards(features, masks, rulebook, send_lists, conv_weight, down_weight, cotangent):
    peers = lax.axis_size("spatial")
    me = lax.axis_index("spatial").astype(jnp.int32)
    x = lax.axis_index("dp").astype(jnp.int32)
    me_s = me.reshape(1)
    sends = send_lists[0, 0].T
    feat = features.reshape(BD, ROWS, LANES)
    cot = cotangent.reshape(BD * 16, LANES)
    mask = masks.reshape(BD, 1, ROWS * EDGE)

    brick = jax.ShapeDtypeStruct((BD, ROWS, LANES), BF16)
    parts = [jax.ShapeDtypeStruct((len(items), SHELL, 128), BF16) for items in all_items()]
    held = pltpu.VMEM((BD + 1, SHELL, 128), BF16)
    own_shape = jax.ShapeDtypeStruct((BD, SHELL, 128), BF16)
    masked, own, *sent = call(pack_kernel, [brick, own_shape, *parts], [me_s, sends, feat, mask], 2, [held])
    recv = exchange(sent, peers)

    entry = rulebook.reshape(BD * 27)
    other = jnp.clip(entry - BD, 0, 2 * peers - 1)
    p = other // 2
    apart = []
    for theirs, ours in zip(region(p), region(me)):
        apart.append(jnp.clip(theirs - ours, -1, 1))
    there = BD + 2 * place(*apart) + other % 2
    idx = jnp.where(entry < BD, entry, jnp.where(entry >= BD + 2 * peers, EMPTY, there)).astype(jnp.int32)
    idx = jnp.clip(idx, 0, EMPTY)

    taps = conv_weight.reshape(3, 3, 3, 64, 64)
    wf = pair_weights(taps, 64)
    wb = pair_weights(taps[:, :, ::-1].transpose(0, 1, 2, 4, 3), 64)
    down = down_weight.reshape(512, 128)
    sel, selt = (jnp.asarray(v, BF16) for v in selections())
    outs = [
        jax.ShapeDtypeStruct((BD * HALF, HALF, LANES), BF16),
        jax.ShapeDtypeStruct((BD, ROWS, LANES), F32),
        jax.ShapeDtypeStruct((BD, SHELL, 128), F32),
        jax.ShapeDtypeStruct((8 * SHELL, 128), F32),
        *parts,
    ]
    scratch = [
        pltpu.VMEM((EXT, SHELL, 128), F32),
        pltpu.VMEM((EXT, SHELL, 128), F32),
        pltpu.VMEM((PADR, PADL), F32),
        pltpu.VMEM((BD * ROWS, 5 * GROUP), BF16),
        pltpu.VMEM((BD * ROWS, LANES), F32),
        pltpu.VMEM((BD * ROWS, LANES), BF16),
        pltpu.VMEM((BD * ROWS, LANES), BF16),
        pltpu.VMEM((BD * PADR, 4 * GROUP), BF16),
        pltpu.VMEM((BD * PADR, PADL), F32),
    ]
    coarse, center, gown, sums, *back = call(
        main_kernel, outs, [idx, me_s, own, masked, mask, cot, sel, selt, wf, wb, down, *recv], 2, scratch, 10**10
    )
    came, near, far = exchange_and_sum(back, sums, me, x, peers)
    [grad] = call(
        last_kernel,
        [brick],
        [me_s, sends, mask, center, gown, *came],
        2,
        [pltpu.VMEM((BD + 1, SHELL, 128), F32)],
    )
    scale = float(lax.axis_size("dp") * peers * BD * EDGE**3) ** (-0.5)
    spot = jnp.stack([x, me % 2])
    conv_sum, down_sum = call(
        lambda *refs: finish_kernel(scale, *refs),
        [jax.ShapeDtypeStruct((27, 64, 64), F32), jax.ShapeDtypeStruct((8, 64, 128), F32)],
        [spot, near, *after([far], grad)],
        1,
        [pltpu.VMEM((8, SHELL, 128), F32)],
    )
    return (
        coarse.reshape(cotangent.shape),
        grad.reshape(features.shape),
        conv_sum,
        down_sum,
    )


def solution(mesh):
    placed = (
        P("dp", "spatial", None, None, None),
        P("dp", "spatial", None),
        P("dp", "spatial", None),
        P("dp", "spatial", None, None),
        P(),
        P(),
        P("dp", "spatial", None, None, None),
    )
    return jax.shard_map(
        shards,
        mesh=mesh,
        in_specs=placed,
        out_specs=(
            P("dp", "spatial", None, None, None),
            P("dp", "spatial", None, None, None),
            P(),
            P(),
        ),
        check_vma=False,
    )
```

```python
import jax
import jax.numpy as jnp
import numpy as np
from jax import lax
from jax.experimental import pallas as pl
from jax.experimental.pallas import tpu as pltpu
from jax.sharding import PartitionSpec as P

F32, BF16 = jnp.float32, jnp.bfloat16
BD = 6
EDGE = 8
HALF = 4
ROWS = EDGE * EDGE
LANES = 512
SHELL = 176
PADR = 112
PADL = 640
EXT = 61
EMPTY = 60
SIDE = 4
GROUP = 9 * 128
VMEM = 58 * 2**20

X_LO, X_HI, Y_LO, Y_HI, Z_AT = 0, 32, 64, 96, 128

PLANE = [(0, 1), (0, -1), (1, 1), (1, 0), (1, -1), (-1, 1), (-1, 0), (-1, -1)]


def slots_of(a, b, c):
    return 2 if abs(a) + abs(b) + abs(c) == 1 else 1


def plane_items(u, w, by):
    a, b, near = u * by[0], w * by[1], by[2]
    own = [(a, b, 0, s) for s in range(slots_of(u, w, 0))]
    return own + [(a, b, near, 0), (a, b, -near, 0)]


def place(a, b, c):
    return 9 * (a + 1) + 3 * (b + 1) + c + 1


def region(d):
    q = d // 16
    return (q % 2) * 2 + q // 2, (d // 4) % 4, d % 4


def steps(d):
    return tuple(1 - 2 * (r % 2) for r in region(d))


def swap_pairs(count, u, w):
    where = {region(d): d for d in range(count)}
    pairs = []
    for d in range(count):
        r, by = region(d), steps(d)
        to = (r[0] + u * by[0], r[1] + w * by[1], r[2])
        if to in where:
            pairs.append((d, where[to]))
    return pairs


def pad_row(x, y):
    if 1 <= y <= 8:
        return x * 8 + y - 1
    base = 80 if y == 0 else 96
    return base + (x - 1 if 1 <= x <= 8 else (8 if x == 0 else 9))


def selections():
    sel = np.zeros((9, 4, 16, PADR), np.float32)
    for dx in range(3):
        for dy in range(3):
            for ox in range(2):
                for oy in range(2):
                    for hx in range(4):
                        for hy in range(4):
                            row = pad_row(2 * hx + ox + dx, 2 * hy + oy + dy)
                            sel[dx * 3 + dy, ox * 2 + oy, hx * 4 + hy, row] = 1
    sel = sel.reshape(9, ROWS, PADR)
    return sel.reshape(9 * ROWS, PADR), sel.transpose(0, 2, 1).reshape(9 * PADR, ROWS)


def dot(a, b, ca=1, cb=0):
    return lax.dot_general(a, b, (((ca,), (cb,)), ((), ())), preferred_element_type=F32)


def iota(shape, dim):
    return lax.broadcasted_iota(jnp.int32, shape, dim)


def spread_mask(voxels, width):
    hit = iota((128, LANES), 1) // width == iota((128, LANES), 0) // (width // 64)
    return dot(voxels, hit.astype(F32).astype(BF16))


def voxel_rows(mask_ref, permuted):
    deep = (iota((LANES, 128), 0) % 8 == iota((LANES, 128), 1)).astype(F32).astype(BF16)
    masks = [mask_ref[b].astype(F32) for b in range(BD)]
    pieces = []
    if permuted:
        row, lane = iota((16, LANES), 0), iota((16, LANES), 1) // 8
        for q in range(4):
            mine = (2 * (row // 4) + q // 2) * 8 + 2 * (row % 4) + q % 2 == lane
            for b in range(BD):
                pieces.append(jnp.where(mine, jnp.broadcast_to(masks[b], (16, LANES)), 0.0))
    else:
        mine = iota((ROWS, LANES), 0) == iota((ROWS, LANES), 1) // 8
        for b in range(BD):
            pieces.append(jnp.where(mine, jnp.broadcast_to(masks[b], (ROWS, LANES)), 0.0))
    return dot(jnp.concatenate(pieces, axis=0).astype(BF16), deep).astype(BF16)


def low_half(shape):
    return iota(shape, len(shape) - 1) < 64


def row_is(row):
    return iota((8, 128), 0) == row


def choice(me_ref, send_ref, a, b, c, s):
    me = me_ref[0]
    q = me // 16
    r0, r1, r2 = (q % 2) * 2 + q // 2 + a, (me // 4) % 4 + b, me % 4 + c
    inside = (r0 >= 0) & (r0 < SIDE) & (r1 >= 0) & (r1 < SIDE) & (r2 >= 0) & (r2 < SIDE)
    to = ((r0 % 2) * 2 + r0 // 2) * 16 + r1 * 4 + r2
    to = jnp.where(inside, to, 0)
    got = send_ref[s, to]
    return jnp.clip(jnp.where(inside, got, BD), 0, BD)


def all_items(by=(1, 1, 1)):
    lists = [plane_items(u, w, by) for u, w in PLANE]
    lists += [[(0, 0, by[2], s) for s in range(2)], [(0, 0, -by[2], s) for s in range(2)]]
    return lists


def received_items(by):
    lists = [[(u * by[0], w * by[1], 0, s) for s in range(slots_of(u, w, 0))] for u, w in PLANE]
    for c in (by[2], -by[2]):
        lists.append([(0, 0, c, s) for s in range(2)] + [(u * by[0], w * by[1], c, 0) for u, w in PLANE])
    return lists


def pack_kernel(me_ref, send_ref, feat_ref, mask_ref, masked_ref, own_ref, *rest):
    outs, held = rest[:10], rest[10]
    pick = iota((16, ROWS), 1) == (iota((16, ROWS), 0) % 8) * 8 + (iota((16, ROWS), 0) // 8) * 7
    pick = pick.astype(F32).astype(BF16)
    voxels = voxel_rows(mask_ref, False)
    for b in range(BD):
        keep = spread_mask(voxels[b * ROWS : (b + 1) * ROWS], 64)
        m = feat_ref[b].astype(F32) * keep
        mb = m.astype(BF16)
        masked_ref[b] = mb
        ys = dot(pick, mb)
        tiles = []
        for block in (m[0:8], m[56:64], ys[0:8], ys[8:16]):
            tiles += [block[:, 128 * q : 128 * (q + 1)] for q in range(4)]
        both = jnp.where(low_half((ROWS, 128)), m[:, 0:128], m[:, 384:512])
        tiles.append(both[8:56])
        shell = jnp.concatenate(tiles, axis=0).astype(BF16)
        own_ref[b] = shell
        held[b] = shell
    held[BD] = jnp.zeros((SHELL, 128), BF16)
    for out, items in zip(outs, all_items(steps(me_ref[0]))):
        for k, item in enumerate(items):
            out[k] = held[choice(me_ref, send_ref, *item)]


def brick_blocks():
    groups = []
    for x, y in ((0, 1), (2, 1), (1, 0), (1, 2)):
        if y == 1:
            first, at = (0, X_HI) if x == 0 else (72, X_LO)
        else:
            first, at = (80, Y_HI) if y == 0 else (96, Y_LO)
        groups.append((first, 9 * x + 3 * y, at))
    return groups


def silu_slope(value, sig):
    return sig * (1.0 + value * (1.0 - sig))


def main_kernel(
    idx_ref, me_ref, own_ref, masked_ref, mask_ref, cot_ref, sel_ref, selt_ref, wf_ref, wb_ref, down_ref, *rest
):
    recv = rest[:10]
    coarse_ref, center_ref, gown_ref, sums_ref = rest[10:14]
    outs = rest[14:24]
    ext, gext, pad, cols, slope, kids, grads, gcols, gpad = rest[24:]
    low8 = low_half((8, 128))

    for b in range(BD):
        ext[b] = own_ref[b].astype(F32)
    ext[EMPTY] = jnp.zeros((SHELL, 128), F32)
    by = steps(me_ref[0])
    for ref, items in zip(recv, received_items(by)):
        for k, (a, b, c, s) in enumerate(items):
            ext[BD + 2 * place(a, b, c) + s] = ref[k].astype(F32)
    gext[...] = jnp.zeros_like(gext)

    @pl.loop(0, BD)
    def _(b):
        base = b * 27

        def src(t, row, size):
            return ext[idx_ref[base + t], row : row + size, :]

        for first, t, at in brick_blocks():
            for q in range(4):
                pad[first : first + 8, 128 * q : 128 * (q + 1)] = src(t + 1, at + 8 * q, 8)
            pad[first : first + 8, 512:640] = jnp.where(low8, src(t + 2, at, 8), src(t, at + 24, 8))
        pad[8:72, 0:512] = masked_ref[b].astype(F32)
        for x in range(8):
            hi_at, lo_at = (X_LO, X_LO + 24) if x == 0 else (X_HI, X_HI + 24) if x == 7 else (Z_AT + 8 * x - 8,) * 2
            pad[8 + 8 * x : 16 + 8 * x, 512:640] = jnp.where(low8, src(14, hi_at, 8), src(12, lo_at, 8))
        for y in (0, 2):
            first = 88 if y == 0 else 104
            row = 7 if y == 0 else 0
            for q in range(5):
                lines = []
                for x in (0, 2):
                    t = 9 * x + 3 * y
                    at = (X_HI if x == 0 else X_LO) + row
                    if q < 4:
                        line = src(t + 1, at + 8 * q, 1)
                    else:
                        line = jnp.where(low_half((1, 128)), src(t + 2, at, 1), src(t, at + 24, 1))
                    lines.append(jnp.broadcast_to(line, (8, 128)))
                pad[first : first + 8, 128 * q : 128 * (q + 1)] = jnp.where(
                    row_is(0), lines[0], jnp.where(row_is(1), lines[1], 0.0)
                )
        turned = pltpu.roll(pad[...], 64, 1).astype(BF16)
        picked = dot(sel_ref[...], turned).astype(BF16)
        for t in range(9):
            for q in range(4):
                rows = picked[t * 64 + q * 16 : t * 64 + q * 16 + 16]
                to = pl.ds(pl.multiple_of(q * 96 + b * 16, 16), 16)
                for k in range(5):
                    cols[to, k * GROUP + t * 128 : k * GROUP + (t + 1) * 128] = rows[:, k * 128 : (k + 1) * 128]

    voxp = voxel_rows(mask_ref, True)
    keep = spread_mask(voxp, 64)
    for p in range(4):
        pre = dot(cols[:, GROUP * p : GROUP * (p + 2)], wf_ref[...])
        kept = keep[:, 128 * p : 128 * (p + 1)]
        pre = pre * kept
        sig = jax.nn.sigmoid(pre)
        slope[:, 128 * p : 128 * (p + 1)] = silu_slope(pre, sig) * kept
        hidden = (pre * sig).astype(BF16)
        for q in range(4):
            kids[p * 96 : (p + 1) * 96, q * 128 : (q + 1) * 128] = hidden[q * 96 : (q + 1) * 96]
    v32 = voxp.astype(F32)
    number = v32[0:96] + v32[96:192] + v32[192:288] + v32[288:384]
    active = (spread_mask(number.astype(BF16), 128) > 0.5).astype(F32)
    pre_out = dot(kids[...], down_ref[...])
    sig = jax.nn.sigmoid(pre_out)
    value = pre_out * sig
    bend = silu_slope(pre_out, sig)
    pieces, parts = [], []
    for p in range(4):
        rows, lanes = slice(96 * p, 96 * (p + 1)), slice(128 * p, 128 * (p + 1))
        pieces.append(value[rows] * active[:, lanes])
        parts.append((cot_ref[:, lanes].astype(F32) * active[:, lanes] * bend[rows]).astype(BF16))
    coarse = jnp.concatenate(pieces, axis=1)
    for k in range(BD * HALF):
        coarse_ref[k] = coarse[HALF * k : HALF * (k + 1)].astype(BF16)
    grad_pre = jnp.concatenate(parts, axis=0)

    back = dot(grad_pre, down_ref[...], 1, 1)
    for p in range(4):
        for q in range(4):
            rows, lanes = slice(96 * q, 96 * (q + 1)), slice(128 * p, 128 * (p + 1))
            part = back[96 * p : 96 * (p + 1), 128 * q : 128 * (q + 1)]
            grads[rows, lanes] = (part * slope[rows, lanes]).astype(BF16)

    down_sum = dot(grad_pre, kids[...], 0, 0)
    for q in range(4):
        sums_ref[896 + 128 * q : 1024 + 128 * q, :] = down_sum[:, 128 * q : 128 * (q + 1)]
    total = None
    for p in range(4):
        term = dot(grads[:, 128 * p : 128 * (p + 1)], cols[:, GROUP * p : GROUP * (p + 2)], 0, 0)
        total = term if total is None else total + term
    third = []
    low64 = low_half((64, 128))
    for t in range(9):
        first = total[:, t * 128 : (t + 1) * 128]
        later = total[:, GROUP + t * 128 : GROUP + (t + 1) * 128]
        mixed = pltpu.roll(jnp.where(low64, later[64:], first[64:]), 64, 1)
        sums_ref[64 * t : 64 * (t + 1), :] = first[:64] + mixed
        third.append(later[:64] + pltpu.roll(later[64:], 64, 1))
    third.append(jnp.zeros((64, 128), F32))
    for m in range(5):
        sums_ref[576 + 64 * m : 640 + 64 * m, :] = jnp.where(
            low64, third[2 * m], pltpu.roll(third[2 * m + 1], 64, 1)
        )

    @pl.loop(0, BD)
    def _(b):
        mine = jnp.concatenate(
            [grads[pl.ds(pl.multiple_of(q * 96 + b * 16, 16), 16), :] for q in range(4)], axis=0
        )
        placed = dot(selt_ref[...], mine).astype(BF16)
        to = pl.ds(pl.multiple_of(b * PADR, 16), PADR)
        for t in range(9):
            for k in range(4):
                gcols[to, k * GROUP + t * 128 : k * GROUP + (t + 1) * 128] = placed[
                    t * PADR : (t + 1) * PADR, k * 128 : (k + 1) * 128
                ]

    for j in range(5):
        lo, hi = max(j - 1, 0), min(j + 1, 4)
        w_lo = GROUP if j == 0 else 0
        w_hi = GROUP if j == 4 else 2 * GROUP
        gpad[:, 128 * j : 128 * (j + 1)] = dot(gcols[:, GROUP * lo : GROUP * hi], wb_ref[w_lo:w_hi, :])

    @pl.loop(0, BD)
    def _(b):
        base = b * 27
        g = pltpu.roll(gpad[pl.ds(pl.multiple_of(b * PADR, 8), PADR), :], PADL - 64, 1)
        center_ref[b] = g[8:72, 0:512]

        def add(t, row, data):
            at = idx_ref[base + t]
            gext[at, row : row + data.shape[0], :] = gext[at, row : row + data.shape[0], :] + data

        for first, t, at in brick_blocks():
            for q in range(4):
                add(t + 1, at + 8 * q, g[first : first + 8, 128 * q : 128 * (q + 1)])
            rim = g[first : first + 8, 512:640]
            add(t + 2, at, jnp.where(low8, rim, 0.0))
            add(t, at + 24, jnp.where(low8, 0.0, rim))
        for x in range(8):
            hi_at, lo_at = (X_LO, X_LO + 24) if x == 0 else (X_HI, X_HI + 24) if x == 7 else (Z_AT + 8 * x - 8,) * 2
            rim = g[8 + 8 * x : 16 + 8 * x, 512:640]
            add(14, hi_at, jnp.where(low8, rim, 0.0))
            add(12, lo_at, jnp.where(low8, 0.0, rim))
        for y in (0, 2):
            first = 88 if y == 0 else 104
            row = 7 if y == 0 else 0
            for n, x in enumerate((0, 2)):
                t = 9 * x + 3 * y
                at = X_HI if x == 0 else X_LO
                for q in range(5):
                    line = jnp.broadcast_to(g[first + n : first + n + 1, 128 * q : 128 * (q + 1)], (8, 128))
                    line = jnp.where(row_is(row), line, 0.0)
                    if q < 4:
                        add(t + 1, at + 8 * q, line)
                    else:
                        add(t + 2, at, jnp.where(low8, line, 0.0))
                        add(t, at + 24, jnp.where(low8, 0.0, line))

    for b in range(BD):
        gown_ref[b] = gext[b]
    for out, items in zip(outs, all_items(by)):
        for k, (a, b, c, s) in enumerate(items):
            out[k] = gext[BD + 2 * place(a, b, c) + s].astype(BF16)


def last_kernel(me_ref, send_ref, mask_ref, center_ref, gown_ref, *rest):
    recv, out_ref, acc = rest[:10], rest[10], rest[11]
    for b in range(BD):
        acc[b] = gown_ref[b]
    acc[BD] = jnp.zeros((SHELL, 128), F32)

    def add(data, *item):
        at = choice(me_ref, send_ref, *item)
        acc[at] = acc[at] + data.astype(F32)

    for ref, items in zip(recv, received_items(steps(me_ref[0]))):
        for k, item in enumerate(items):
            add(ref[k], *item)
    low8 = low_half((8, 128))
    voxels = voxel_rows(mask_ref, False)
    for b in range(BD):
        keep = spread_mask(voxels[b * ROWS : (b + 1) * ROWS], 64)
        lines = []
        for x in range(8):
            blocks = []
            for q in range(4):
                v = center_ref[b, 8 * x : 8 * x + 8, 128 * q : 128 * (q + 1)]
                y_lo = acc[b, Y_LO + 8 * q + x : Y_LO + 8 * q + x + 1, :]
                y_hi = acc[b, Y_HI + 8 * q + x : Y_HI + 8 * q + x + 1, :]
                v = v + jnp.where(row_is(0), jnp.broadcast_to(y_lo, (8, 128)), 0.0)
                v = v + jnp.where(row_is(7), jnp.broadcast_to(y_hi, (8, 128)), 0.0)
                if x == 0:
                    v = v + acc[b, X_LO + 8 * q : X_LO + 8 * q + 8, :]
                if x == 7:
                    v = v + acc[b, X_HI + 8 * q : X_HI + 8 * q + 8, :]
                if 1 <= x <= 6 and q in (0, 3):
                    z = acc[b, Z_AT + 8 * x - 8 : Z_AT + 8 * x, :]
                    v = v + (jnp.where(low8, z, 0.0) if q == 0 else jnp.where(low8, 0.0, z))
                blocks.append(v)
            lines.append(jnp.concatenate(blocks, axis=1))
        dense = jnp.concatenate(lines, axis=0)
        out_ref[b] = (dense * keep).astype(BF16)


def finish_kernel(scale, place_ref, near_ref, far_ref, conv_ref, down_ref, held):
    x, core = place_ref[0], place_ref[1]
    for k in range(4):
        at = jnp.bitwise_xor(x, k)
        held[core * 4 + at] = near_ref[k].astype(F32) * scale
        held[(1 - core) * 4 + at] = far_ref[k].astype(F32) * scale
    full = jnp.concatenate([held[k] for k in range(8)], axis=0)
    for t in range(9):
        turned = full[64 * t : 64 * (t + 1)].T
        conv_ref[3 * t] = turned[:64]
        conv_ref[3 * t + 1] = turned[64:]
    for m in range(5):
        turned = full[576 + 64 * m : 640 + 64 * m].T
        conv_ref[6 * m + 2] = turned[:64]
        if m < 4:
            conv_ref[6 * m + 5] = turned[64:]
    for q in range(4):
        turned = full[896 + 128 * q : 1024 + 128 * q].T
        down_ref[2 * q] = turned[:64]
        down_ref[2 * q + 1] = turned[64:]


def call(kernel, outs, args, smem, scratch=(), flops=0):
    spec_s = pl.BlockSpec(memory_space=pltpu.SMEM)
    spec_v = pl.BlockSpec(memory_space=pltpu.VMEM)
    moved = sum(int(np.prod(v.shape)) * v.dtype.itemsize for v in (*args, *outs))
    return pl.pallas_call(
        kernel,
        out_shape=outs,
        in_specs=[spec_s] * smem + [spec_v] * (len(args) - smem),
        out_specs=[spec_v] * len(outs),
        scratch_shapes=list(scratch),
        compiler_params=pltpu.CompilerParams(vmem_limit_bytes=VMEM),
        cost_estimate=pl.CostEstimate(flops=flops, bytes_accessed=moved, transcendentals=0),
    )(*args)


def exchange_plane(parts, peers):
    return [lax.ppermute(v, "spatial", swap_pairs(peers, a, b)) for (a, b), v in zip(PLANE, parts)]


def exchange_along(got, parts, peers):
    swaps = [[(d, d ^ 1) for d in range(peers)]]
    swaps += [[(d, d + 1 if d % SIDE == 1 else d - 1) for d in range(peers) if d % SIDE in (1, 2)]]
    along = []
    for n in (1, 0):
        pieces = [parts[8 + n]]
        for v in got:
            at = v.shape[0] - 2 + n
            pieces.append(v[at : at + 1])
        along.append(lax.ppermute(jnp.concatenate(pieces, axis=0), "spatial", swaps[n]))
    return [*got, along[1], along[0]]


def exchange(parts, peers):
    return exchange_along(exchange_plane(parts, peers), parts, peers)


def pair_weights(taps, width):
    zero = jnp.zeros((3, 3, 1, width, width), taps.dtype)
    first = jnp.concatenate([taps, zero], axis=2)
    second = jnp.concatenate([zero, taps], axis=2)
    both = jnp.stack([first, second], axis=4).reshape(9, 2, 2 * width, 2 * width)
    return both.transpose(1, 0, 2, 3).reshape(2 * GROUP, 2 * width)


def after(values, earlier):
    return lax.optimization_barrier((tuple(values), earlier))[0]


def exchange_and_sum(parts, sums, me, x, peers):
    core = me % 2
    got = {}

    def plane(lo, hi, earlier=None):
        keys = PLANE[lo:hi]
        ins = [parts[PLANE.index(k)] for k in keys]
        if earlier is not None:
            ins = after(ins, earlier)
        for k, v in zip(keys, ins):
            got[k] = lax.ppermute(v, "spatial", swap_pairs(peers, *k))

    def swap(v, bit):
        return lax.ppermute(v, "spatial", [(d, d ^ bit) for d in range(peers)])

    def swap_x(v, bit):
        return lax.ppermute(v, "dp", [(d, d ^ bit) for d in range(4)])

    def one_of(v, at):
        return lax.dynamic_index_in_dim(v, at, 0, keepdims=False)

    def pairs(w, bits):
        all_of = [w.astype(F32)] + [swap(w, bit).astype(F32) for bit in bits]
        while len(all_of) > 1:
            all_of = [all_of[i] + all_of[i + 1] for i in range(0, len(all_of), 2)]
        return all_of[0].astype(BF16)

    halves = sums.reshape(2, 4, SHELL, 128)
    plane(0, 4)
    mine = one_of(halves, core) + swap(one_of(halves, 1 - core).astype(BF16), 1).astype(F32)
    small = mine.astype(BF16)
    away = [one_of(small, jnp.bitwise_xor(x, k)) for k in (1, 2, 3)]
    plane(4, 6, tuple(away))
    v = one_of(mine, x)
    for k in (1, 2, 3):
        v = v + swap_x(away[k - 1], k).astype(F32)
    w = v.astype(BF16)
    plane(6, 8, w)
    w = pairs(w, (16, 32, 48))
    w = pairs(w, (2,))
    w = pairs(w, (4, 8, 12))
    near = jnp.stack([w] + [swap_x(w, k) for k in (1, 2, 3)])
    came = exchange_along([got[k] for k in PLANE], parts, peers)
    return came, near, swap(near, 1)


def shards(features, masks, rulebook, send_lists, conv_weight, down_weight, cotangent):
    peers = lax.axis_size("spatial")
    me = lax.axis_index("spatial").astype(jnp.int32)
    x = lax.axis_index("dp").astype(jnp.int32)
    me_s = me.reshape(1)
    sends = send_lists[0, 0].T
    feat = features.reshape(BD, ROWS, LANES)
    cot = cotangent.reshape(BD * 16, LANES)
    mask = masks.reshape(BD, 1, ROWS * EDGE)

    brick = jax.ShapeDtypeStruct((BD, ROWS, LANES), BF16)
    parts = [jax.ShapeDtypeStruct((len(items), SHELL, 128), BF16) for items in all_items()]
    held = pltpu.VMEM((BD + 1, SHELL, 128), BF16)
    own_shape = jax.ShapeDtypeStruct((BD, SHELL, 128), BF16)
    masked, own, *sent = call(pack_kernel, [brick, own_shape, *parts], [me_s, sends, feat, mask], 2, [held])
    recv = exchange(sent, peers)

    entry = rulebook.reshape(BD * 27)
    other = jnp.clip(entry - BD, 0, 2 * peers - 1)
    p = other // 2
    apart = []
    for theirs, ours in zip(region(p), region(me)):
        apart.append(jnp.clip(theirs - ours, -1, 1))
    there = BD + 2 * place(*apart) + other % 2
    idx = jnp.where(entry < BD, entry, jnp.where(entry >= BD + 2 * peers, EMPTY, there)).astype(jnp.int32)
    idx = jnp.clip(idx, 0, EMPTY)

    taps = conv_weight.reshape(3, 3, 3, 64, 64)
    wf = pair_weights(taps, 64)
    wb = pair_weights(taps[:, :, ::-1].transpose(0, 1, 2, 4, 3), 64)
    down = down_weight.reshape(512, 128)
    sel, selt = (jnp.asarray(v, BF16) for v in selections())
    outs = [
        jax.ShapeDtypeStruct((BD * HALF, HALF, LANES), BF16),
        jax.ShapeDtypeStruct((BD, ROWS, LANES), F32),
        jax.ShapeDtypeStruct((BD, SHELL, 128), F32),
        jax.ShapeDtypeStruct((8 * SHELL, 128), F32),
        *parts,
    ]
    scratch = [
        pltpu.VMEM((EXT, SHELL, 128), F32),
        pltpu.VMEM((EXT, SHELL, 128), F32),
        pltpu.VMEM((PADR, PADL), F32),
        pltpu.VMEM((BD * ROWS, 5 * GROUP), BF16),
        pltpu.VMEM((BD * ROWS, LANES), F32),
        pltpu.VMEM((BD * ROWS, LANES), BF16),
        pltpu.VMEM((BD * ROWS, LANES), BF16),
        pltpu.VMEM((BD * PADR, 4 * GROUP), BF16),
        pltpu.VMEM((BD * PADR, PADL), F32),
    ]
    coarse, center, gown, sums, *back = call(
        main_kernel, outs, [idx, me_s, own, masked, mask, cot, sel, selt, wf, wb, down, *recv], 2, scratch, 10**10
    )
    came, near, far = exchange_and_sum(back, sums, me, x, peers)
    [grad] = call(
        last_kernel,
        [brick],
        [me_s, sends, mask, center, gown, *came],
        2,
        [pltpu.VMEM((BD + 1, SHELL, 128), F32)],
    )
    scale = float(lax.axis_size("dp") * peers * BD * EDGE**3) ** (-0.5)
    spot = jnp.stack([x, me % 2])
    conv_sum, down_sum = call(
        lambda *refs: finish_kernel(scale, *refs),
        [jax.ShapeDtypeStruct((27, 64, 64), F32), jax.ShapeDtypeStruct((8, 64, 128), F32)],
        [spot, near, *after([far], grad)],
        1,
        [pltpu.VMEM((8, SHELL, 128), F32)],
    )
    return (
        coarse.reshape(cotangent.shape),
        grad.reshape(features.shape),
        conv_sum,
        down_sum,
    )


def solution(mesh):
    placed = (
        P("dp", "spatial", None, None, None),
        P("dp", "spatial", None),
        P("dp", "spatial", None),
        P("dp", "spatial", None, None),
        P(),
        P(),
        P("dp", "spatial", None, None, None),
    )
    return jax.shard_map(
        shards,
        mesh=mesh,
        in_specs=placed,
        out_specs=(
            P("dp", "spatial", None, None, None),
            P("dp", "spatial", None, None, None),
            P(),
            P(),
        ),
        check_vma=False,
    )
```

```python
import jax
import jax.numpy as jnp
import numpy as np
from jax import lax
from jax.experimental import pallas as pl
from jax.experimental.pallas import tpu as pltpu
from jax.sharding import PartitionSpec as P

F32, BF16 = jnp.float32, jnp.bfloat16
BD = 6
EDGE = 8
HALF = 4
ROWS = EDGE * EDGE
LANES = 512
SHELL = 176
PADR = 112
PADL = 640
EXT = 61
EMPTY = 60
SIDE = 4
GROUP = 9 * 128
VMEM = 58 * 2**20

X_LO, X_HI, Y_LO, Y_HI, Z_AT = 0, 32, 64, 96, 128

PLANE = [(0, 1), (0, -1), (1, 1), (1, 0), (1, -1), (-1, 1), (-1, 0), (-1, -1)]


def slots_of(a, b, c):
    return 2 if abs(a) + abs(b) + abs(c) == 1 else 1


def plane_items(u, w, by):
    a, b, near = u * by[0], w * by[1], by[2]
    own = [(a, b, 0, s) for s in range(slots_of(u, w, 0))]
    return own + [(a, b, near, 0), (a, b, -near, 0)]


def place(a, b, c):
    return 9 * (a + 1) + 3 * (b + 1) + c + 1


def region(d):
    q = d // 16
    return (q % 2) * 2 + q // 2, (d // 4) % 4, d % 4


def steps(d):
    return tuple(1 - 2 * (r % 2) for r in region(d))


def swap_pairs(count, u, w):
    where = {region(d): d for d in range(count)}
    pairs = []
    for d in range(count):
        r, by = region(d), steps(d)
        to = (r[0] + u * by[0], r[1] + w * by[1], r[2])
        if to in where:
            pairs.append((d, where[to]))
    return pairs


def pad_row(x, y):
    if 1 <= y <= 8:
        return x * 8 + y - 1
    base = 80 if y == 0 else 96
    return base + (x - 1 if 1 <= x <= 8 else (8 if x == 0 else 9))


def selections():
    sel = np.zeros((9, 4, 16, PADR), np.float32)
    for dx in range(3):
        for dy in range(3):
            for ox in range(2):
                for oy in range(2):
                    for hx in range(4):
                        for hy in range(4):
                            row = pad_row(2 * hx + ox + dx, 2 * hy + oy + dy)
                            sel[dx * 3 + dy, ox * 2 + oy, hx * 4 + hy, row] = 1
    sel = sel.reshape(9, ROWS, PADR)
    return sel.reshape(9 * ROWS, PADR), sel.transpose(0, 2, 1).reshape(9 * PADR, ROWS)


def dot(a, b, ca=1, cb=0):
    return lax.dot_general(a, b, (((ca,), (cb,)), ((), ())), preferred_element_type=F32)


def iota(shape, dim):
    return lax.broadcasted_iota(jnp.int32, shape, dim)


def spread_mask(voxels, width):
    hit = iota((128, LANES), 1) // width == iota((128, LANES), 0) // (width // 64)
    return dot(voxels, hit.astype(F32).astype(BF16))


def voxel_rows(mask_ref, permuted):
    deep = (iota((LANES, 128), 0) % 8 == iota((LANES, 128), 1)).astype(F32).astype(BF16)
    masks = [mask_ref[b].astype(F32) for b in range(BD)]
    pieces = []
    if permuted:
        row, lane = iota((16, LANES), 0), iota((16, LANES), 1) // 8
        for q in range(4):
            mine = (2 * (row // 4) + q // 2) * 8 + 2 * (row % 4) + q % 2 == lane
            for b in range(BD):
                pieces.append(jnp.where(mine, jnp.broadcast_to(masks[b], (16, LANES)), 0.0))
    else:
        mine = iota((ROWS, LANES), 0) == iota((ROWS, LANES), 1) // 8
        for b in range(BD):
            pieces.append(jnp.where(mine, jnp.broadcast_to(masks[b], (ROWS, LANES)), 0.0))
    return dot(jnp.concatenate(pieces, axis=0).astype(BF16), deep).astype(BF16)


def low_half(shape):
    return iota(shape, len(shape) - 1) < 64


def row_is(row):
    return iota((8, 128), 0) == row


def choice(me_ref, send_ref, a, b, c, s):
    me = me_ref[0]
    q = me // 16
    r0, r1, r2 = (q % 2) * 2 + q // 2 + a, (me // 4) % 4 + b, me % 4 + c
    inside = (r0 >= 0) & (r0 < SIDE) & (r1 >= 0) & (r1 < SIDE) & (r2 >= 0) & (r2 < SIDE)
    to = ((r0 % 2) * 2 + r0 // 2) * 16 + r1 * 4 + r2
    to = jnp.where(inside, to, 0)
    got = send_ref[s, to]
    return jnp.clip(jnp.where(inside, got, BD), 0, BD)


def all_items(by=(1, 1, 1)):
    lists = [plane_items(u, w, by) for u, w in PLANE]
    lists += [[(0, 0, by[2], s) for s in range(2)], [(0, 0, -by[2], s) for s in range(2)]]
    return lists


def received_items(by):
    lists = [[(u * by[0], w * by[1], 0, s) for s in range(slots_of(u, w, 0))] for u, w in PLANE]
    for c in (by[2], -by[2]):
        lists.append([(0, 0, c, s) for s in range(2)] + [(u * by[0], w * by[1], c, 0) for u, w in PLANE])
    return lists


def pack_kernel(me_ref, send_ref, feat_ref, mask_ref, masked_ref, own_ref, *rest):
    outs, held = rest[:10], rest[10]
    pick = iota((16, ROWS), 1) == (iota((16, ROWS), 0) % 8) * 8 + (iota((16, ROWS), 0) // 8) * 7
    pick = pick.astype(F32).astype(BF16)
    voxels = voxel_rows(mask_ref, False)
    for b in range(BD):
        keep = spread_mask(voxels[b * ROWS : (b + 1) * ROWS], 64)
        m = feat_ref[b].astype(F32) * keep
        mb = m.astype(BF16)
        masked_ref[b] = mb
        ys = dot(pick, mb)
        tiles = []
        for block in (m[0:8], m[56:64], ys[0:8], ys[8:16]):
            tiles += [block[:, 128 * q : 128 * (q + 1)] for q in range(4)]
        both = jnp.where(low_half((ROWS, 128)), m[:, 0:128], m[:, 384:512])
        tiles.append(both[8:56])
        shell = jnp.concatenate(tiles, axis=0).astype(BF16)
        own_ref[b] = shell
        held[b] = shell
    held[BD] = jnp.zeros((SHELL, 128), BF16)
    for out, items in zip(outs, all_items(steps(me_ref[0]))):
        for k, item in enumerate(items):
            out[k] = held[choice(me_ref, send_ref, *item)]


def brick_blocks():
    groups = []
    for x, y in ((0, 1), (2, 1), (1, 0), (1, 2)):
        if y == 1:
            first, at = (0, X_HI) if x == 0 else (72, X_LO)
        else:
            first, at = (80, Y_HI) if y == 0 else (96, Y_LO)
        groups.append((first, 9 * x + 3 * y, at))
    return groups


def silu_slope(value, sig):
    return sig * (1.0 + value * (1.0 - sig))


def main_kernel(
    idx_ref, me_ref, own_ref, masked_ref, mask_ref, cot_ref, sel_ref, selt_ref, wf_ref, wb_ref, down_ref, *rest
):
    recv = rest[:10]
    coarse_ref, center_ref, gown_ref, kept_ref, away_ref = rest[10:15]
    outs = rest[15:25]
    ext, gext, pad, cols, slope, kids, grads, gcols, gpad, sums_ref = rest[25:]
    low8 = low_half((8, 128))

    for b in range(BD):
        ext[b] = own_ref[b].astype(F32)
    ext[EMPTY] = jnp.zeros((SHELL, 128), F32)
    by = steps(me_ref[0])
    for ref, items in zip(recv, received_items(by)):
        for k, (a, b, c, s) in enumerate(items):
            ext[BD + 2 * place(a, b, c) + s] = ref[k].astype(F32)
    gext[...] = jnp.zeros_like(gext)

    @pl.loop(0, BD)
    def _(b):
        base = b * 27

        def src(t, row, size):
            return ext[idx_ref[base + t], row : row + size, :]

        for first, t, at in brick_blocks():
            for q in range(4):
                pad[first : first + 8, 128 * q : 128 * (q + 1)] = src(t + 1, at + 8 * q, 8)
            pad[first : first + 8, 512:640] = jnp.where(low8, src(t + 2, at, 8), src(t, at + 24, 8))
        pad[8:72, 0:512] = masked_ref[b].astype(F32)
        for x in range(8):
            hi_at, lo_at = (X_LO, X_LO + 24) if x == 0 else (X_HI, X_HI + 24) if x == 7 else (Z_AT + 8 * x - 8,) * 2
            pad[8 + 8 * x : 16 + 8 * x, 512:640] = jnp.where(low8, src(14, hi_at, 8), src(12, lo_at, 8))
        for y in (0, 2):
            first = 88 if y == 0 else 104
            row = 7 if y == 0 else 0
            for q in range(5):
                lines = []
                for x in (0, 2):
                    t = 9 * x + 3 * y
                    at = (X_HI if x == 0 else X_LO) + row
                    if q < 4:
                        line = src(t + 1, at + 8 * q, 1)
                    else:
                        line = jnp.where(low_half((1, 128)), src(t + 2, at, 1), src(t, at + 24, 1))
                    lines.append(jnp.broadcast_to(line, (8, 128)))
                pad[first : first + 8, 128 * q : 128 * (q + 1)] = jnp.where(
                    row_is(0), lines[0], jnp.where(row_is(1), lines[1], 0.0)
                )
        turned = pltpu.roll(pad[...], 64, 1).astype(BF16)
        picked = dot(sel_ref[...], turned).astype(BF16)
        for t in range(9):
            for q in range(4):
                rows = picked[t * 64 + q * 16 : t * 64 + q * 16 + 16]
                to = pl.ds(pl.multiple_of(q * 96 + b * 16, 16), 16)
                for k in range(5):
                    cols[to, k * GROUP + t * 128 : k * GROUP + (t + 1) * 128] = rows[:, k * 128 : (k + 1) * 128]

    voxp = voxel_rows(mask_ref, True)
    keep = spread_mask(voxp, 64)
    for p in range(4):
        pre = dot(cols[:, GROUP * p : GROUP * (p + 2)], wf_ref[...])
        kept = keep[:, 128 * p : 128 * (p + 1)]
        pre = pre * kept
        sig = jax.nn.sigmoid(pre)
        slope[:, 128 * p : 128 * (p + 1)] = silu_slope(pre, sig) * kept
        hidden = (pre * sig).astype(BF16)
        for q in range(4):
            kids[p * 96 : (p + 1) * 96, q * 128 : (q + 1) * 128] = hidden[q * 96 : (q + 1) * 96]
    v32 = voxp.astype(F32)
    number = v32[0:96] + v32[96:192] + v32[192:288] + v32[288:384]
    active = (spread_mask(number.astype(BF16), 128) > 0.5).astype(F32)
    pre_out = dot(kids[...], down_ref[...])
    sig = jax.nn.sigmoid(pre_out)
    value = pre_out * sig
    bend = silu_slope(pre_out, sig)
    pieces, parts = [], []
    for p in range(4):
        rows, lanes = slice(96 * p, 96 * (p + 1)), slice(128 * p, 128 * (p + 1))
        pieces.append(value[rows] * active[:, lanes])
        parts.append((cot_ref[:, lanes].astype(F32) * active[:, lanes] * bend[rows]).astype(BF16))
    coarse = jnp.concatenate(pieces, axis=1)
    for k in range(BD * HALF):
        coarse_ref[k] = coarse[HALF * k : HALF * (k + 1)].astype(BF16)
    grad_pre = jnp.concatenate(parts, axis=0)

    back = dot(grad_pre, down_ref[...], 1, 1)
    for p in range(4):
        for q in range(4):
            rows, lanes = slice(96 * q, 96 * (q + 1)), slice(128 * p, 128 * (p + 1))
            part = back[96 * p : 96 * (p + 1), 128 * q : 128 * (q + 1)]
            grads[rows, lanes] = (part * slope[rows, lanes]).astype(BF16)

    down_sum = dot(grad_pre, kids[...], 0, 0)
    for q in range(4):
        sums_ref[896 + 128 * q : 1024 + 128 * q, :] = down_sum[:, 128 * q : 128 * (q + 1)]
    total = None
    for p in range(4):
        term = dot(grads[:, 128 * p : 128 * (p + 1)], cols[:, GROUP * p : GROUP * (p + 2)], 0, 0)
        total = term if total is None else total + term
    third = []
    low64 = low_half((64, 128))
    for t in range(9):
        first = total[:, t * 128 : (t + 1) * 128]
        later = total[:, GROUP + t * 128 : GROUP + (t + 1) * 128]
        mixed = pltpu.roll(jnp.where(low64, later[64:], first[64:]), 64, 1)
        sums_ref[64 * t : 64 * (t + 1), :] = first[:64] + mixed
        third.append(later[:64] + pltpu.roll(later[64:], 64, 1))
    third.append(jnp.zeros((64, 128), F32))
    for m in range(5):
        sums_ref[576 + 64 * m : 640 + 64 * m, :] = jnp.where(
            low64, third[2 * m], pltpu.roll(third[2 * m + 1], 64, 1)
        )

    half, core = 4 * SHELL, me_ref[0] % 2
    kept_ref[...] = sums_ref[pl.ds(pl.multiple_of(core * half, 8), half), :]
    away_ref[...] = sums_ref[pl.ds(pl.multiple_of((1 - core) * half, 8), half), :].astype(BF16)

    @pl.loop(0, BD)
    def _(b):
        mine = jnp.concatenate(
            [grads[pl.ds(pl.multiple_of(q * 96 + b * 16, 16), 16), :] for q in range(4)], axis=0
        )
        placed = dot(selt_ref[...], mine).astype(BF16)
        to = pl.ds(pl.multiple_of(b * PADR, 16), PADR)
        for t in range(9):
            for k in range(4):
                gcols[to, k * GROUP + t * 128 : k * GROUP + (t + 1) * 128] = placed[
                    t * PADR : (t + 1) * PADR, k * 128 : (k + 1) * 128
                ]

    for j in range(5):
        lo, hi = max(j - 1, 0), min(j + 1, 4)
        w_lo = GROUP if j == 0 else 0
        w_hi = GROUP if j == 4 else 2 * GROUP
        gpad[:, 128 * j : 128 * (j + 1)] = dot(gcols[:, GROUP * lo : GROUP * hi], wb_ref[w_lo:w_hi, :])

    @pl.loop(0, BD)
    def _(b):
        base = b * 27
        g = pltpu.roll(gpad[pl.ds(pl.multiple_of(b * PADR, 8), PADR), :], PADL - 64, 1)
        center_ref[b] = g[8:72, 0:512]

        def add(t, row, data):
            at = idx_ref[base + t]
            gext[at, row : row + data.shape[0], :] = gext[at, row : row + data.shape[0], :] + data

        for first, t, at in brick_blocks():
            for q in range(4):
                add(t + 1, at + 8 * q, g[first : first + 8, 128 * q : 128 * (q + 1)])
            rim = g[first : first + 8, 512:640]
            add(t + 2, at, jnp.where(low8, rim, 0.0))
            add(t, at + 24, jnp.where(low8, 0.0, rim))
        for x in range(8):
            hi_at, lo_at = (X_LO, X_LO + 24) if x == 0 else (X_HI, X_HI + 24) if x == 7 else (Z_AT + 8 * x - 8,) * 2
            rim = g[8 + 8 * x : 16 + 8 * x, 512:640]
            add(14, hi_at, jnp.where(low8, rim, 0.0))
            add(12, lo_at, jnp.where(low8, 0.0, rim))
        for y in (0, 2):
            first = 88 if y == 0 else 104
            row = 7 if y == 0 else 0
            for n, x in enumerate((0, 2)):
                t = 9 * x + 3 * y
                at = X_HI if x == 0 else X_LO
                for q in range(5):
                    line = jnp.broadcast_to(g[first + n : first + n + 1, 128 * q : 128 * (q + 1)], (8, 128))
                    line = jnp.where(row_is(row), line, 0.0)
                    if q < 4:
                        add(t + 1, at + 8 * q, line)
                    else:
                        add(t + 2, at, jnp.where(low8, line, 0.0))
                        add(t, at + 24, jnp.where(low8, 0.0, line))

    for b in range(BD):
        gown_ref[b] = gext[b]
    for out, items in zip(outs, all_items(by)):
        for k, (a, b, c, s) in enumerate(items):
            out[k] = gext[BD + 2 * place(a, b, c) + s].astype(BF16)


def last_kernel(me_ref, send_ref, mask_ref, center_ref, gown_ref, *rest):
    recv, out_ref, acc = rest[:10], rest[10], rest[11]
    for b in range(BD):
        acc[b] = gown_ref[b]
    acc[BD] = jnp.zeros((SHELL, 128), F32)

    def add(data, *item):
        at = choice(me_ref, send_ref, *item)
        acc[at] = acc[at] + data.astype(F32)

    for ref, items in zip(recv, received_items(steps(me_ref[0]))):
        for k, item in enumerate(items):
            add(ref[k], *item)
    low8 = low_half((8, 128))
    voxels = voxel_rows(mask_ref, False)
    for b in range(BD):
        keep = spread_mask(voxels[b * ROWS : (b + 1) * ROWS], 64)
        lines = []
        for x in range(8):
            blocks = []
            for q in range(4):
                v = center_ref[b, 8 * x : 8 * x + 8, 128 * q : 128 * (q + 1)]
                y_lo = acc[b, Y_LO + 8 * q + x : Y_LO + 8 * q + x + 1, :]
                y_hi = acc[b, Y_HI + 8 * q + x : Y_HI + 8 * q + x + 1, :]
                v = v + jnp.where(row_is(0), jnp.broadcast_to(y_lo, (8, 128)), 0.0)
                v = v + jnp.where(row_is(7), jnp.broadcast_to(y_hi, (8, 128)), 0.0)
                if x == 0:
                    v = v + acc[b, X_LO + 8 * q : X_LO + 8 * q + 8, :]
                if x == 7:
                    v = v + acc[b, X_HI + 8 * q : X_HI + 8 * q + 8, :]
                if 1 <= x <= 6 and q in (0, 3):
                    z = acc[b, Z_AT + 8 * x - 8 : Z_AT + 8 * x, :]
                    v = v + (jnp.where(low8, z, 0.0) if q == 0 else jnp.where(low8, 0.0, z))
                blocks.append(v)
            lines.append(jnp.concatenate(blocks, axis=1))
        dense = jnp.concatenate(lines, axis=0)
        out_ref[b] = (dense * keep).astype(BF16)


def finish_kernel(scale, place_ref, near_ref, far_ref, conv_ref, down_ref, held):
    x, core = place_ref[0], place_ref[1]
    for k in range(4):
        at = jnp.bitwise_xor(x, k)
        held[core * 4 + at] = near_ref[k].astype(F32) * scale
        held[(1 - core) * 4 + at] = far_ref[k].astype(F32) * scale
    full = jnp.concatenate([held[k] for k in range(8)], axis=0)
    for t in range(9):
        turned = full[64 * t : 64 * (t + 1)].T
        conv_ref[3 * t] = turned[:64]
        conv_ref[3 * t + 1] = turned[64:]
    for m in range(5):
        turned = full[576 + 64 * m : 640 + 64 * m].T
        conv_ref[6 * m + 2] = turned[:64]
        if m < 4:
            conv_ref[6 * m + 5] = turned[64:]
    for q in range(4):
        turned = full[896 + 128 * q : 1024 + 128 * q].T
        down_ref[2 * q] = turned[:64]
        down_ref[2 * q + 1] = turned[64:]


def call(kernel, outs, args, smem, scratch=(), flops=0):
    spec_s = pl.BlockSpec(memory_space=pltpu.SMEM)
    spec_v = pl.BlockSpec(memory_space=pltpu.VMEM)
    moved = sum(int(np.prod(v.shape)) * v.dtype.itemsize for v in (*args, *outs))
    return pl.pallas_call(
        kernel,
        out_shape=outs,
        in_specs=[spec_s] * smem + [spec_v] * (len(args) - smem),
        out_specs=[spec_v] * len(outs),
        scratch_shapes=list(scratch),
        compiler_params=pltpu.CompilerParams(vmem_limit_bytes=VMEM),
        cost_estimate=pl.CostEstimate(flops=flops, bytes_accessed=moved, transcendentals=0),
    )(*args)


def exchange_plane(parts, peers):
    return [lax.ppermute(v, "spatial", swap_pairs(peers, a, b)) for (a, b), v in zip(PLANE, parts)]


def exchange_along(got, parts, peers):
    swaps = [[(d, d ^ 1) for d in range(peers)]]
    swaps += [[(d, d + 1 if d % SIDE == 1 else d - 1) for d in range(peers) if d % SIDE in (1, 2)]]
    along = []
    for n in (1, 0):
        pieces = [parts[8 + n]]
        for v in got:
            at = v.shape[0] - 2 + n
            pieces.append(v[at : at + 1])
        along.append(lax.ppermute(jnp.concatenate(pieces, axis=0), "spatial", swaps[n]))
    return [*got, along[1], along[0]]


def exchange(parts, peers):
    return exchange_along(exchange_plane(parts, peers), parts, peers)


def pair_weights(taps, width):
    zero = jnp.zeros((3, 3, 1, width, width), taps.dtype)
    first = jnp.concatenate([taps, zero], axis=2)
    second = jnp.concatenate([zero, taps], axis=2)
    both = jnp.stack([first, second], axis=4).reshape(9, 2, 2 * width, 2 * width)
    return both.transpose(1, 0, 2, 3).reshape(2 * GROUP, 2 * width)


def after(values, earlier):
    return lax.optimization_barrier((tuple(values), earlier))[0]


def exchange_and_sum(parts, kept, sent, x, peers):
    got = {}

    def plane(lo, hi, earlier=None):
        keys = PLANE[lo:hi]
        ins = [parts[PLANE.index(k)] for k in keys]
        if earlier is not None:
            ins = after(ins, earlier)
        for k, v in zip(keys, ins):
            got[k] = lax.ppermute(v, "spatial", swap_pairs(peers, *k))

    def swap(v, bit):
        return lax.ppermute(v, "spatial", [(d, d ^ bit) for d in range(peers)])

    def swap_x(v, bit):
        return lax.ppermute(v, "dp", [(d, d ^ bit) for d in range(4)])

    def one_of(v, at):
        return lax.dynamic_index_in_dim(v, at, 0, keepdims=False)

    def pairs(w, bits):
        all_of = [w.astype(F32)] + [swap(w, bit).astype(F32) for bit in bits]
        while len(all_of) > 1:
            all_of = [all_of[i] + all_of[i + 1] for i in range(0, len(all_of), 2)]
        return all_of[0].astype(BF16)

    shape = (4, SHELL, 128)
    plane(0, 4)
    mine = kept.reshape(shape) + swap(sent.reshape(shape), 1).astype(F32)
    small = mine.astype(BF16)
    away = [one_of(small, jnp.bitwise_xor(x, k)) for k in (1, 2, 3)]
    plane(4, 6, tuple(away))
    v = one_of(mine, x)
    for k in (1, 2, 3):
        v = v + swap_x(away[k - 1], k).astype(F32)
    w = v.astype(BF16)
    plane(6, 8, w)
    w = pairs(w, (16, 32, 48))
    w = pairs(w, (2,))
    w = pairs(w, (4, 8, 12))
    near = jnp.stack([w] + [swap_x(w, k) for k in (1, 2, 3)])
    came = exchange_along([got[k] for k in PLANE], parts, peers)
    return came, near, swap(near, 1)


def shards(features, masks, rulebook, send_lists, conv_weight, down_weight, cotangent):
    peers = lax.axis_size("spatial")
    me = lax.axis_index("spatial").astype(jnp.int32)
    x = lax.axis_index("dp").astype(jnp.int32)
    me_s = me.reshape(1)
    sends = send_lists[0, 0].T
    feat = features.reshape(BD, ROWS, LANES)
    cot = cotangent.reshape(BD * 16, LANES)
    mask = masks.reshape(BD, 1, ROWS * EDGE)

    brick = jax.ShapeDtypeStruct((BD, ROWS, LANES), BF16)
    parts = [jax.ShapeDtypeStruct((len(items), SHELL, 128), BF16) for items in all_items()]
    held = pltpu.VMEM((BD + 1, SHELL, 128), BF16)
    own_shape = jax.ShapeDtypeStruct((BD, SHELL, 128), BF16)
    masked, own, *sent = call(pack_kernel, [brick, own_shape, *parts], [me_s, sends, feat, mask], 2, [held])
    recv = exchange(sent, peers)

    entry = rulebook.reshape(BD * 27)
    other = jnp.clip(entry - BD, 0, 2 * peers - 1)
    p = other // 2
    apart = []
    for theirs, ours in zip(region(p), region(me)):
        apart.append(jnp.clip(theirs - ours, -1, 1))
    there = BD + 2 * place(*apart) + other % 2
    idx = jnp.where(entry < BD, entry, jnp.where(entry >= BD + 2 * peers, EMPTY, there)).astype(jnp.int32)
    idx = jnp.clip(idx, 0, EMPTY)

    taps = conv_weight.reshape(3, 3, 3, 64, 64)
    wf = pair_weights(taps, 64)
    wb = pair_weights(taps[:, :, ::-1].transpose(0, 1, 2, 4, 3), 64)
    down = down_weight.reshape(512, 128)
    sel, selt = (jnp.asarray(v, BF16) for v in selections())
    outs = [
        jax.ShapeDtypeStruct((BD * HALF, HALF, LANES), BF16),
        jax.ShapeDtypeStruct((BD, ROWS, LANES), F32),
        jax.ShapeDtypeStruct((BD, SHELL, 128), F32),
        jax.ShapeDtypeStruct((4 * SHELL, 128), F32),
        jax.ShapeDtypeStruct((4 * SHELL, 128), BF16),
        *parts,
    ]
    scratch = [
        pltpu.VMEM((EXT, SHELL, 128), F32),
        pltpu.VMEM((EXT, SHELL, 128), F32),
        pltpu.VMEM((PADR, PADL), F32),
        pltpu.VMEM((BD * ROWS, 5 * GROUP), BF16),
        pltpu.VMEM((BD * ROWS, LANES), F32),
        pltpu.VMEM((BD * ROWS, LANES), BF16),
        pltpu.VMEM((BD * ROWS, LANES), BF16),
        pltpu.VMEM((BD * PADR, 4 * GROUP), BF16),
        pltpu.VMEM((BD * PADR, PADL), F32),
        pltpu.VMEM((8 * SHELL, 128), F32),
    ]
    coarse, center, gown, kept, away, *back = call(
        main_kernel, outs, [idx, me_s, own, masked, mask, cot, sel, selt, wf, wb, down, *recv], 2, scratch, 10**10
    )
    came, near, far = exchange_and_sum(back, kept, away, x, peers)
    [grad] = call(
        last_kernel,
        [brick],
        [me_s, sends, mask, center, gown, *came],
        2,
        [pltpu.VMEM((BD + 1, SHELL, 128), F32)],
    )
    scale = float(lax.axis_size("dp") * peers * BD * EDGE**3) ** (-0.5)
    spot = jnp.stack([x, me % 2])
    conv_sum, down_sum = call(
        lambda *refs: finish_kernel(scale, *refs),
        [jax.ShapeDtypeStruct((27, 64, 64), F32), jax.ShapeDtypeStruct((8, 64, 128), F32)],
        [spot, near, *after([far], grad)],
        1,
        [pltpu.VMEM((8, SHELL, 128), F32)],
    )
    return (
        coarse.reshape(cotangent.shape),
        grad.reshape(features.shape),
        conv_sum,
        down_sum,
    )


def solution(mesh):
    placed = (
        P("dp", "spatial", None, None, None),
        P("dp", "spatial", None),
        P("dp", "spatial", None),
        P("dp", "spatial", None, None),
        P(),
        P(),
        P("dp", "spatial", None, None, None),
    )
    return jax.shard_map(
        shards,
        mesh=mesh,
        in_specs=placed,
        out_specs=(
            P("dp", "spatial", None, None, None),
            P("dp", "spatial", None, None, None),
            P(),
            P(),
        ),
        check_vma=False,
    )
```
